256 devices in a mesh: rows: 64 (over z, y, core), nbr: 4 (over x).
Axes of the slice: x: 4, y: 4, z: 8, core: 2. Of those that a mesh axis runs over, the one named last changes fastest.
Arguments:
- expression: bfloat16 [1024, 128, 128], P('rows'), may hold values from -80 to 80
- nbr_owner: int32 [4, 1024, 4], replicated, may hold values from 0 to 63, all different within a row; in each aligned block of 16 rows (0 to 15, 16 to 31, ..., all dimensions but the last counted through in order) at most 2 rows name the same one
- nbr_slot: int32 [4, 1024, 4], replicated, may hold values from 0 to 15
Outputs:
- intersection_tiles: float32 [1024, 16, 128, 128], P('rows', 'nbr')
The draws below stay inside these ranges and needn't reach their ends.
Inputs may be any that keep to these rules, and one draw needn't show every extreme that they name: `nbr_owner`: each row (n, b) names 4 different owners. Within the 16 rows b of one device's bands for one n, no owner is named more than 2 times, and in some such groups an owner is named exactly 2 times.
All inputs are finite; a program needn't handle non-finite values.
Results may differ from the reference program's by a relative error of at most 0.01.
Values may be sent and summed in bfloat16 or wider, within the bound.
A program may use at most 128 MiB of HBM per device.

```python
import math
import jax
import jax.numpy as jnp
import numpy as np
from jax import lax

B = 128
S = 128
BLK_DEV = 16
KN = 4
K = 16
BLOCKS = 1024
CAP = 2
N_ROWS = 64
N_NBR = 4


def draw_expression(key, part):
    subkeys = jax.random.split(key, 5)
    gene_count = BLOCKS * B
    module = jax.random.randint(subkeys[0], (gene_count,), 0, 32)
    signs = (2 * jax.random.randint(subkeys[1], (gene_count,), 0, 2) - 1).astype(jnp.float32)
    loading = 0.85 * signs
    spread = jnp.exp(jax.random.uniform(subkeys[2], (gene_count, 1), jnp.float32, 0.0, 2.302585))
    factors = jnp.clip(jax.random.normal(subkeys[3], (32, S), jnp.float32), -4.0, 4.0)
    noise_part = jnp.clip(jax.random.normal(subkeys[4], (gene_count, S), jnp.float32), -4.0, 4.0)
    shared = factors[module]
    rows_value = loading[:, None] * shared + jnp.sqrt(1.0 - loading * loading)[:, None] * noise_part
    return (spread * rows_value).reshape(BLOCKS, B, S).astype(jnp.bfloat16)


def set_ends(result, key, least, high):
    longest = result.shape.index(max(result.shape))
    spots = []
    for shift in (0, 1):
        where = [jax.random.randint(jax.random.fold_in(key, axis), (), 0, length) for axis, length in enumerate(result.shape)]
        where[longest] = (where[longest] + shift) % result.shape[longest]
        spots.append(tuple(where))
    return result.at[spots[0]].set(least).at[spots[1]].set(high)


def deal_out(rng, own, number, rows, number_of, top, bound, lean):
    order = jax.random.permutation(rng, number_of)
    packed, ordinary = portions_of(number_of, rows * top, bound, lean, True), portions_of(number_of, rows * top, bound, lean, False)
    places = jnp.arange(number_of)

    def named(sizes, rotation):
        used = int((sizes > 0).sum())
        fixed = max(1, used // 4)
        shifted = fixed + (places - fixed + rotation * (used - fixed)) % max(1, number_of - fixed)
        return jnp.zeros((number_of,), jnp.int32).at[order[jnp.where(places < fixed, places, shifted)]].set(jnp.asarray(sizes, jnp.int32))

    sizes = jnp.where(number % 4 == 0, named(packed, number // 4), named(ordinary, number - number // 4 - 1))
    mixed = jax.random.permutation(jax.random.fold_in(own, 3), number_of)
    source_of, taker = mixed[0:number_of // 2 * 2:2], mixed[1:number_of // 2 * 2:2]
    margin = jnp.minimum(sizes[source_of] - 1, bound - sizes[taker]) // 2
    margin = jnp.where((source_of == order[0]) | (taker == order[0]) | (sizes[taker] == 0), 0, jnp.maximum(margin, 0))
    shifted = jax.random.randint(jax.random.fold_in(own, 4), (number_of // 2,), 0, 1 << 20) % (margin + 1)
    sizes = sizes.at[source_of].add(-shifted).at[taker].add(shifted)
    members = jnp.searchsorted(jnp.cumsum(sizes), jnp.arange(rows * top), side="right").astype(jnp.int32)
    table = members.reshape(top, rows).T
    table = table[jax.random.permutation(jax.random.fold_in(own, 1), rows)]
    rotation = jax.random.randint(jax.random.fold_in(own, 2), (rows, 1), 0, top)
    return jnp.take_along_axis(table, (jnp.arange(top)[None, :] + rotation) % top, axis=1)


def portions_of(count, total, reach, skew, full):
    portions = [(1 << 20) // math.isqrt(grade ** skew) + 1 for grade in range(1, count + 1)]
    largest = reach if full else min(reach, max(-(-total // count), total * portions[0] // sum(portions)))
    least = 1 if total - largest >= count - 1 else 0
    holding, surplus = [largest] + [least] * (count - 1), total - largest - least * (count - 1)
    while surplus > 0:
        candidates = [i for i in range(1, count) if holding[i] < largest] or [i for i in range(1, count) if holding[i] < reach]
        pool, remaining = sum([portions[i] for i in candidates]), surplus
        for i in candidates:
            addition = min(reach - holding[i], max(1, remaining * portions[i] // pool), surplus)
            holding[i] = holding[i] + addition
            surplus = surplus - addition
    return np.array(holding)


def setup_inputs(seed: int = 0) -> dict:
    keys = jax.random.split(jax.random.key(seed), 4)
    expression = draw_expression(jax.random.fold_in(keys[3], 71), 0)
    nbr_owner_keys = jax.random.split(jax.random.fold_in(keys[1], 1), N_NBR * BLOCKS // BLK_DEV)
    nbr_owner_turns = jax.random.permutation(jax.random.fold_in(keys[1], 3), N_NBR * BLOCKS // BLK_DEV)
    nbr_owner = jax.vmap(lambda own, number: deal_out(jax.random.fold_in(keys[1], 2), own, number, BLK_DEV, N_ROWS, KN, CAP, 2))(nbr_owner_keys, nbr_owner_turns).reshape((N_NBR, BLOCKS, KN))
    nbr_slot = set_ends(jax.random.randint(keys[2], (N_NBR, BLOCKS, KN), 0, BLK_DEV), jax.random.fold_in(keys[2], 1), 0, BLK_DEV - 1).astype(jnp.int32)
    return dict(expression=expression, nbr_owner=nbr_owner, nbr_slot=nbr_slot)


def standardize(blocks):
    values = blocks.astype(jnp.float32)
    centred = values - lax.optimization_barrier(jnp.mean(values, axis=-1, keepdims=True))
    inverse_norm = lax.rsqrt(lax.optimization_barrier(jnp.sum(centred * centred, axis=-1, keepdims=True)) + 1e-06)
    return (centred * inverse_norm).astype(jnp.bfloat16)

def power_twelve(correlation):
    base = 0.5 + 0.5 * correlation
    second = base * base
    fourth = second * second
    eighth = fourth * fourth
    return eighth * fourth

def soft_adjacency(left_rows, right_rows, same_block):
    correlation = jnp.einsum('uvs,cjs->uvcj', left_rows.astype(jnp.float32), right_rows.astype(jnp.float32))
    soft_value = power_twelve(correlation)
    diagonal = jnp.eye(left_rows.shape[1], dtype=bool)
    zeroed = same_block[:, None, :, None] & diagonal[None, :, None, :]
    return jnp.where(zeroed, 0.0, soft_value).astype(jnp.bfloat16)

def reference(expression, nbr_owner, nbr_slot):
    zscores = standardize(expression)
    band_lists = jnp.transpose(nbr_owner * BLK_DEV + nbr_slot, (1, 0, 2)).reshape(BLOCKS, K).astype(jnp.int32)
    band_ids = jnp.arange(BLOCKS, dtype=jnp.int32)
    position = jnp.arange(K, dtype=jnp.int32)
    earlier = position[None, :] < position[:, None]
    repeated = jnp.any((band_lists[:, :, None] == band_lists[:, None, :]) & earlier[None], axis=2)
    weights = ((band_lists != band_ids[:, None]) & jnp.logical_not(repeated)).astype(jnp.float32)

    def row_block(band_index):
        near_ids = band_lists[band_index]
        stacked = jnp.concatenate([zscores[band_index][None], zscores[near_ids]], axis=0)
        same_block = jnp.concatenate([jnp.ones((1,), bool), near_ids == band_index])[None, :]
        return soft_adjacency(zscores[band_index][None], stacked, same_block)[0]

    def degree(band_index):
        band_row = row_block(band_index).astype(jnp.float32)
        full_weights = jnp.concatenate([jnp.ones((1,), jnp.float32), weights[band_index]])
        return lax.optimization_barrier(jnp.sum(band_row * full_weights[None, :, None], axis=(1, 2)))
    degrees = lax.map(degree, band_ids)

    def intersection(band_index):
        band_row = row_block(band_index)
        near_ids = band_lists[band_index]
        neighbours = zscores[near_ids]
        pair_tiles = soft_adjacency(neighbours, neighbours, near_ids[:, None] == near_ids[None, :]).astype(jnp.float32)
        self_row = band_row[:, 0, :].astype(jnp.float32)
        list_row = band_row[:, 1:, :].astype(jnp.float32)
        self_term = jnp.einsum('iv,vcj->icj', self_row, list_row)
        lead = (list_row * weights[band_index][None, :, None]).reshape(B, N_NBR, KN, B)
        grouped = pair_tiles.reshape(N_NBR, KN, B, K, B)
        parts = jnp.einsum('inuv,nuvcj->nicj', lead, grouped)
        first_mask = (jnp.arange(N_NBR, dtype=jnp.int32) == 0).astype(jnp.float32)
        parts = parts + first_mask[:, None, None, None] * self_term[None]
        parts = parts.astype(jnp.bfloat16).astype(jnp.float32)
        shared = lax.optimization_barrier(jnp.sum(parts, axis=0))
        numerator = shared + list_row
        denominator = jnp.minimum(degrees[band_index][:, None, None], degrees[near_ids][None, :, :]) + 1.0 - list_row
        return jnp.transpose(numerator / denominator, (1, 0, 2))
    return lax.map(intersection, band_ids)
```

```python
import heapq

import jax
import jax.numpy as jnp
from jax import lax
from jax.experimental import pallas as pl
from jax.experimental.pallas import tpu as pltpu
from jax.sharding import PartitionSpec as P

MESH = pl.DeviceIdType.MESH
BLOCK = 128
BANDS = 16
LIST = 16
OWN = 4
ZS, YS, XS = 8, 4, 4
CHIPS = ZS * YS
SHARD = BANDS * BLOCK
HALF = CHIPS * SHARD
PIECE = {"A": 704, "B": 672}
START = {"A": 0, "B": 704, "C": 704 + 672}
WIDTH = LIST * BLOCK + BLOCK
OWN_WIDTH = OWN * BLOCK
NT = (((1,), (1,)), ((), ()))


def piece_rows(kind, part):
    rows = PIECE["A" if kind == "A" else "B"]
    return rows if part == "f" else rows // 2


def next_sends(kind, part, dy, dz):
    sends = []
    if kind == "C":
        return sends
    first, second = part in "fa", part in "fb"
    along_z, along_y = [], []
    if 0 <= dz < 3:
        along_z.append(("z+", kind, part, dy, dz + 1))
    if dz == 3 and first:
        along_z.append(("z+", kind, "a", dy, 4))
    if -3 < dz <= 0:
        along_z.append(("z-", kind, part, dy, dz - 1))
    if dz == -3 and second:
        along_z.append(("z-", kind, "b", dy, -4))
    if dy == 0:
        along_y += [("y+", kind, part, 1, dz), ("y-", kind, part, -1, dz)]
    if dy == 1 and first:
        along_y.append(("y+", kind, "a", 2, dz))
    if dy == -1 and second:
        along_y.append(("y-", kind, "b", -2, dz))
    if kind == "A":
        sends += along_y if dz == 0 else []
        sends += along_z
    else:
        sends += along_z if dy == 0 else []
        sends += along_y
        if dy or dz:
            sends.append(("x+" if dz % 2 == 0 else "x-", "C", part, dy, dz))
    return sends


def gather_plan():
    free, heap, order, count, clock = {}, [], [], 0, 0.0
    for kind in ("B", "A"):
        heapq.heappush(heap, (0.0, count, (None, kind, "f", 0, 0)))
        count += 1
    while heap:
        time, _, event = heapq.heappop(heap)
        order.append(event)
        clock = max(clock, time) + 0.1
        for send in next_sends(*event[1:]):
            began = max(free.get(send[0], 0.0), clock)
            free[send[0]] = began + 2 * piece_rows(send[1], send[2]) * 256 / 115e3
            heapq.heappush(heap, (free[send[0]] + 2.5, count, send))
            count += 1
    return order


PLAN = gather_plan()
ARRIVALS = {event: number for number, event in enumerate(PLAN)}


def standardize_into(x_ref, z_all, mine):
    def one(i, carry):
        values = x_ref[i].astype(jnp.float32)
        centred = values - jnp.mean(values, axis=-1, keepdims=True)
        inverse = lax.rsqrt(jnp.sum(centred * centred, axis=-1, keepdims=True) + 1e-06)
        z_all[pl.ds(pl.multiple_of(mine + i * BLOCK, BLOCK), BLOCK), :] = (centred * inverse).astype(
            jnp.bfloat16
        )
        return carry

    lax.fori_loop(0, BANDS, one, 0)


def off_diagonal(dtype):
    i = lax.broadcasted_iota(jnp.int32, (BLOCK, BLOCK), 0)
    j = lax.broadcasted_iota(jnp.int32, (BLOCK, BLOCK), 1)
    return jnp.where(i == j, 0.0, 1.0).astype(dtype)


def block_of(z_all, block):
    return z_all[pl.ds(block * BLOCK, BLOCK), :]


def lead_band(b, my_block, block_ref, weight_ref, same_ref, z_all, lead, own_tiles):
    band = block_of(z_all, my_block + b)
    left = band * jnp.bfloat16(0.5)
    at = pl.ds(pl.multiple_of(b * BLOCK, BLOCK), BLOCK)
    apart = off_diagonal(jnp.float32)
    total = jnp.zeros((BLOCK, BLOCK), jnp.float32)
    for begin, end in ((0, 5), (5, 9), (9, 13), (13, 17)):
        right = [
            band if u == 0 else block_of(z_all, block_ref[b, u - 1]) for u in range(begin, end)
        ]
        base = 0.5 + lax.dot_general(
            left, jnp.concatenate(right, axis=0), NT, preferred_element_type=jnp.float32
        )
        second = base * base
        fourth = second * second
        soft = fourth * fourth * fourth
        for u in range(begin, end):
            tile = soft[:, (u - begin) * BLOCK : (u - begin + 1) * BLOCK]
            if u == 0:
                tile = tile * apart
            else:
                if u <= OWN:
                    tile = tile * (1.0 - same_ref[b, u - 1] * (1.0 - apart))
                    own_tiles[at, (u - 1) * BLOCK : u * BLOCK] = tile.astype(jnp.bfloat16)
                tile = tile * weight_ref[b, u - 1]
            lead[at, u * BLOCK : (u + 1) * BLOCK] = tile.astype(jnp.bfloat16)
            total = total + tile
    return jnp.sum(jnp.transpose(total), axis=0, keepdims=True)


def shared_band(b, block_ref, z_all, lead, own_tiles, pair):
    at = pl.ds(pl.multiple_of(b * BLOCK, BLOCK), BLOCK)
    own = [block_of(z_all, block_ref[b, c]) for c in range(OWN)]
    right = jnp.concatenate(own, axis=0) * jnp.bfloat16(0.5)
    apart = off_diagonal(jnp.bfloat16)
    links = own_tiles[at, :]
    pair[0:BLOCK, :] = links
    for u in range(0, LIST, 2):
        left = jnp.concatenate([block_of(z_all, block_ref[b, u + i]) for i in (0, 1)], axis=0)
        base = 0.5 + lax.dot_general(left, right, NT, preferred_element_type=jnp.float32)
        second = base * base
        fourth = (second * second).astype(jnp.bfloat16)
        soft = fourth * fourth * fourth
        top = (u + 1) * BLOCK
        pair[top : top + 2 * BLOCK, :] = soft
        if u < OWN:
            for i in (0, 1):
                c = u + i
                pair[top + i * BLOCK : top + (i + 1) * BLOCK, c * BLOCK : (c + 1) * BLOCK] = (
                    soft[i * BLOCK : (i + 1) * BLOCK, c * BLOCK : (c + 1) * BLOCK] * apart
                )
    shared = jnp.dot(lead[at, :], pair[...], preferred_element_type=jnp.float32)
    return shared + links.astype(jnp.float32)


def kernel(
    x_ref, block_ref, weight_ref, same_ref,
    sum_out, link_out, degree_out,
    z_all, lead, own_tiles, sums, degrees, pair,
    piece_recv, piece_send, core_recv, core_send, degree_recv, degree_send, out_sem,
):
    row = lax.axis_index("rows")
    plane = lax.axis_index("nbr")
    core, chip = row % 2, row // 2
    y, z = chip % YS, chip // YS
    odd = plane % 2

    def device(to_z, to_y):
        return (((to_z + ZS) % ZS * YS + (to_y + YS) % YS) * 2 + core, plane)

    links = {
        "z+": device(z + 1, y), "z-": device(z - 1, y),
        "y+": device(z, y + 1), "y-": device(z, y - 1),
        "x+": (row, (plane + 1) % XS), "x-": (row, (plane + XS - 1) % XS),
    }
    other = (chip * 2 + 1 - core, plane)
    barrier = pltpu.get_barrier_semaphore()
    for neighbour in list(links.values()) + [other]:
        pl.semaphore_signal(barrier, inc=1, device_id=neighbour, device_id_type=MESH)
    mine = core * HALF + chip * SHARD
    standardize_into(x_ref, z_all, mine)
    pl.semaphore_wait(barrier, 7)

    starts = {
        "A": START["A"],
        "B": START["B"] + odd * (START["C"] - START["B"]),
        "C": START["C"] - odd * (START["C"] - START["B"]),
    }

    def rows_at(kind, part, dy, dz):
        owner = (z - dz + ZS) % ZS * YS + (y - dy + YS) % YS
        rows = piece_rows(kind, part)
        first = core * HALF + owner * SHARD + starts[kind] + (rows if part == "b" else 0)
        return z_all.at[pl.ds(pl.multiple_of(first, 16), rows)]

    def copy(ref, send, recv, to):
        return pltpu.make_async_remote_copy(
            src_ref=ref, dst_ref=ref, send_sem=send, recv_sem=recv, device_id=to, device_id_type=MESH
        )

    shard = z_all.at[pl.ds(pl.multiple_of(mine, SHARD), SHARD)]
    sent_rows = 0
    for event in PLAN:
        link, kind, part, dy, dz = event
        ref = rows_at(kind, part, dy, dz)
        if link is not None:
            copy(ref, piece_send, piece_recv.at[ARRIVALS[event]], links[link]).wait_recv()
        for send in next_sends(kind, part, dy, dz):
            src = rows_at(kind, send[2], dy, dz)
            sent_rows += piece_rows(kind, send[2])
            copy(src, piece_send, piece_recv.at[ARRIVALS[send]], links[send[0]]).start()
        if link is not None:
            copy(ref, core_send, core_recv, other).start()
        elif kind == "A":
            copy(shard, core_send, core_recv, other).start()

    def drain(sem, first, rows):
        ref = z_all.at[pl.ds(first, rows)]
        pltpu.make_async_copy(ref, ref, sem).wait()

    drain(core_recv, pl.multiple_of((1 - core) * HALF, HALF), HALF)

    column = core * (CHIPS * BANDS) + y * (ZS * BANDS)
    my_degrees = column + z * BANDS

    def lead_step(b, carry):
        degrees[pl.ds(my_degrees + b, 1), :] = lead_band(
            b, mine // BLOCK, block_ref, weight_ref, same_ref, z_all, lead, own_tiles
        )
        return carry

    lax.fori_loop(0, BANDS, lead_step, 0)
    link_copy = pltpu.make_async_copy(own_tiles, link_out, out_sem.at[1])
    link_copy.start()

    def along_z(dz, part):
        rows = BANDS if part == "f" else BANDS // 2
        first = column + (z - dz + ZS) % ZS * BANDS + (rows if part == "b" else 0)
        return degrees.at[pl.ds(pl.multiple_of(first, 8), rows)]

    def along_y(dy, part):
        rows = ZS * BANDS if part == "f" else ZS * BANDS // 2
        first = (
            core * (CHIPS * BANDS) + (y - dy + YS) % YS * (ZS * BANDS) + (rows if part == "b" else 0)
        )
        return degrees.at[pl.ds(pl.multiple_of(first, 8), rows)]

    def hop(number, ref, link):
        return copy(ref, degree_send.at[number], degree_recv.at[number], links[link])

    def passes(number):
        if number < 3:
            d = number
            return [
                (hop(2 * d, along_z(d, "f"), "z+"), hop(2 * d, along_z(d + 1, "f"), "z+")),
                (hop(2 * d + 1, along_z(-d, "f"), "z-"), hop(2 * d + 1, along_z(-d - 1, "f"), "z-")),
            ]
        if number == 3:
            return [
                (hop(6, along_z(3, "a"), "z+"), hop(6, along_z(4, "a"), "z+")),
                (hop(7, along_z(-3, "b"), "z-"), hop(7, along_z(-4, "b"), "z-")),
            ]
        if number == 4:
            return [
                (hop(8, along_y(0, "f"), "y+"), hop(8, along_y(1, "f"), "y+")),
                (hop(9, along_y(0, "f"), "y-"), hop(9, along_y(-1, "f"), "y-")),
            ]
        if number == 5:
            return [
                (hop(10, along_y(1, "a"), "y+"), hop(10, along_y(2, "a"), "y+")),
                (hop(11, along_y(-1, "b"), "y-"), hop(11, along_y(-2, "b"), "y-")),
            ]
        part = degrees.at[pl.ds(pl.multiple_of(core * (CHIPS * BANDS), CHIPS * BANDS), CHIPS * BANDS)]
        back = degrees.at[
            pl.ds(pl.multiple_of((1 - core) * (CHIPS * BANDS), CHIPS * BANDS), CHIPS * BANDS)
        ]
        return [
            (copy(part, degree_send.at[12], degree_recv.at[12], other),
             copy(back, degree_send.at[12], degree_recv.at[12], other)),
        ]

    rounds = 7

    def exchange(number):
        if number > 0:
            for sent, came in passes(number - 1):
                sent.wait_send()
                came.wait_recv()
        if number < rounds:
            for sent, _ in passes(number):
                sent.start()

    def shared_step(b, carry):
        for number in range(rounds):
            pl.when(b == 2 * number)(lambda number=number: exchange(number))
        numerator = shared_band(b, block_ref, z_all, lead, own_tiles, pair)
        for c in range(OWN):
            sums[b, c] = numerator[:, c * BLOCK : (c + 1) * BLOCK]
        pltpu.make_async_copy(sums.at[b], sum_out.at[b], out_sem.at[0]).start()
        return carry

    lax.fori_loop(0, BANDS, shared_step, 0)
    exchange(rounds)
    degree_copy = pltpu.make_async_copy(degrees, degree_out, out_sem.at[2])
    degree_copy.start()
    pltpu.make_async_copy(sums, sum_out, out_sem.at[0]).wait()
    link_copy.wait()
    degree_copy.wait()
    drain(piece_send, 0, sent_rows)
    drain(core_send, 0, HALF)


def divide(spot_ref, sum_ref, link_ref, degree_ref, out_ref):
    b = pl.program_id(0)
    first = spot_ref[BANDS * OWN] + b
    own_row = degree_ref[pl.ds(first, 1), :]
    own = jnp.transpose(jnp.broadcast_to(own_row, (BLOCK, BLOCK)))
    for c in range(OWN):
        near = degree_ref[pl.ds(spot_ref[b * OWN + c], 1), :]
        link = link_ref[:, c * BLOCK : (c + 1) * BLOCK].astype(jnp.float32)
        out_ref[0, c] = sum_ref[0, c] / (jnp.minimum(own, near) + 1.0 - link)


def per_device(expression, nbr_owner, nbr_slot):
    row = lax.axis_index("rows")
    plane = lax.axis_index("nbr")
    owner = lax.dynamic_slice_in_dim(nbr_owner, row * BANDS, BANDS, 1)
    slot = lax.dynamic_slice_in_dim(nbr_slot, row * BANDS, BANDS, 1)

    def own_first(part):
        turned = jnp.stack([lax.dynamic_index_in_dim(part, (plane + i) % XS, 0, False) for i in range(XS)])
        return jnp.transpose(turned, (1, 0, 2)).reshape(BANDS, LIST)

    owner, slot = own_first(owner), own_first(slot)
    core, chip = owner % 2, owner // 2
    block = core * (CHIPS * BANDS) + chip * BANDS + slot
    ids = owner * BANDS + slot
    same = ids == (row * BANDS + jnp.arange(BANDS, dtype=jnp.int32))[:, None]
    position = jnp.arange(LIST, dtype=jnp.int32)
    earlier = position[None, :] < position[:, None]
    repeated = jnp.any((ids[:, :, None] == ids[:, None, :]) & earlier[None], axis=2)
    weights = (~same & ~repeated).astype(jnp.float32)
    spot = core * (CHIPS * BANDS) + (chip % YS) * (ZS * BANDS) + chip // YS * BANDS + slot
    my_chip = row // 2
    first = (row % 2) * (CHIPS * BANDS) + (my_chip % YS) * (ZS * BANDS) + my_chip // YS * BANDS
    spots = jnp.concatenate([spot[:, :OWN].reshape(-1), first[None]])

    sums, link, degrees = pl.pallas_call(
        kernel,
        out_shape=(
            jax.ShapeDtypeStruct((BANDS, OWN, BLOCK, BLOCK), jnp.float32),
            jax.ShapeDtypeStruct((SHARD, OWN_WIDTH), jnp.bfloat16),
            jax.ShapeDtypeStruct((2 * CHIPS * BANDS, BLOCK), jnp.float32),
        ),
        in_specs=[pl.BlockSpec(memory_space=pltpu.VMEM)]
        + [pl.BlockSpec(memory_space=pltpu.SMEM)] * 3,
        out_specs=(pl.BlockSpec(memory_space=pl.ANY),) * 3,
        scratch_shapes=[
            pltpu.VMEM((2 * HALF, BLOCK), jnp.bfloat16),
            pltpu.VMEM((SHARD, WIDTH), jnp.bfloat16),
            pltpu.VMEM((SHARD, OWN_WIDTH), jnp.bfloat16),
            pltpu.VMEM((BANDS, OWN, BLOCK, BLOCK), jnp.float32),
            pltpu.VMEM((2 * CHIPS * BANDS, BLOCK), jnp.float32),
            pltpu.VMEM((WIDTH, OWN_WIDTH), jnp.bfloat16),
            pltpu.SemaphoreType.DMA((len(PLAN),)),
            pltpu.SemaphoreType.DMA,
            pltpu.SemaphoreType.DMA,
            pltpu.SemaphoreType.DMA,
            pltpu.SemaphoreType.DMA((13,)),
            pltpu.SemaphoreType.DMA((13,)),
            pltpu.SemaphoreType.DMA((3,)),
        ],
        compiler_params=pltpu.CompilerParams(
            collective_id=0, has_side_effects=True, vmem_limit_bytes=60 * 2**20
        ),
    )(expression, block, weights, same[:, :OWN].astype(jnp.float32))

    return pl.pallas_call(
        divide,
        out_shape=jax.ShapeDtypeStruct((BANDS, OWN, BLOCK, BLOCK), jnp.float32),
        grid_spec=pltpu.PrefetchScalarGridSpec(
            num_scalar_prefetch=1,
            grid=(BANDS,),
            in_specs=[
                pl.BlockSpec((1, OWN, BLOCK, BLOCK), lambda b, _: (b, 0, 0, 0)),
                pl.BlockSpec((BLOCK, OWN_WIDTH), lambda b, _: (b, 0)),
                pl.BlockSpec((2 * CHIPS * BANDS, BLOCK), lambda b, _: (0, 0)),
            ],
            out_specs=pl.BlockSpec((1, OWN, BLOCK, BLOCK), lambda b, _: (b, 0, 0, 0)),
        ),
    )(spots, sums, link, degrees)


def solution(mesh):
    return jax.shard_map(
        per_device,
        mesh=mesh,
        in_specs=(P("rows", None, None), P(), P()),
        out_specs=P("rows", "nbr", None, None),
        check_vma=False,
    )
```

```python
import heapq

import jax
import jax.numpy as jnp
from jax import lax
from jax.experimental import pallas as pl
from jax.experimental.pallas import tpu as pltpu
from jax.sharding import PartitionSpec as P

MESH = pl.DeviceIdType.MESH
BLOCK = 128
BANDS = 16
LIST = 16
OWN = 4
ZS, YS, XS = 8, 4, 4
CHIPS = ZS * YS
SHARD = BANDS * BLOCK
HALF = CHIPS * SHARD
PIECE = {"A": 640, "B": 704}
START = {"A": 0, "B": 640, "C": 640 + 704}
WIDTH = LIST * BLOCK + BLOCK
OWN_WIDTH = OWN * BLOCK
NT = (((1,), (1,)), ((), ()))


def piece_rows(kind):
    return PIECE["A" if kind == "A" else "B"] // 2


def next_sends(kind, part, dy, dz):
    sends = []
    if kind == "C":
        return sends
    along_z, along_y = [], []
    if 0 <= dz < 3:
        along_z.append(("z+", kind, part, dy, dz + 1))
    if dz == 3 and part == "a":
        along_z.append(("z+", kind, part, dy, 4))
    if -3 < dz <= 0:
        along_z.append(("z-", kind, part, dy, dz - 1))
    if dz == -3 and part == "b":
        along_z.append(("z-", kind, part, dy, -4))
    if dy == 0:
        along_y += [("y+", kind, part, 1, dz), ("y-", kind, part, -1, dz)]
    if dy == 1 and part == "a":
        along_y.append(("y+", kind, part, 2, dz))
    if dy == -1 and part == "b":
        along_y.append(("y-", kind, part, -2, dz))
    if kind == "A":
        sends += along_y if dz == 0 else []
        sends += along_z
    else:
        sends += along_z if dy == 0 else []
        sends += along_y
        if dy or dz:
            sends.append(("x+" if dz % 2 == 0 else "x-", "C", part, dy, dz))
    return sends


def gather_plan():
    free, heap, order, count, clock = {}, [], [], 0, 0.0
    for kind, part in (("B", "a"), ("B", "b"), ("A", "a"), ("A", "b")):
        heapq.heappush(heap, (0.0, count, (None, kind, part, 0, 0)))
        count += 1
    while heap:
        time, _, event = heapq.heappop(heap)
        order.append(event)
        clock = max(clock, time) + 0.1
        for send in next_sends(*event[1:]):
            began = max(free.get(send[0], 0.0), clock)
            free[send[0]] = began + 2 * piece_rows(send[1]) * 256 / 95e3
            heapq.heappush(heap, (free[send[0]] + 3.2, count, send))
            count += 1
    return order


PLAN = gather_plan()
ARRIVALS = {event: number for number, event in enumerate(PLAN)}


def standardize_into(x_ref, z_all, mine):
    def one(i, carry):
        values = x_ref[i].astype(jnp.float32)
        centred = values - jnp.mean(values, axis=-1, keepdims=True)
        inverse = lax.rsqrt(jnp.sum(centred * centred, axis=-1, keepdims=True) + 1e-06)
        z_all[pl.ds(pl.multiple_of(mine + i * BLOCK, BLOCK), BLOCK), :] = (centred * inverse).astype(
            jnp.bfloat16
        )
        return carry

    lax.fori_loop(0, BANDS, one, 0)


def off_diagonal(dtype):
    i = lax.broadcasted_iota(jnp.int32, (BLOCK, BLOCK), 0)
    j = lax.broadcasted_iota(jnp.int32, (BLOCK, BLOCK), 1)
    return jnp.where(i == j, 0.0, 1.0).astype(dtype)


def block_of(z_all, block):
    return z_all[pl.ds(block * BLOCK, BLOCK), :]


def lead_band(b, my_block, block_ref, weight_ref, same_ref, z_all, lead, own_tiles):
    band = block_of(z_all, my_block + b)
    left = band * jnp.bfloat16(0.5)
    at = pl.ds(pl.multiple_of(b * BLOCK, BLOCK), BLOCK)
    apart = off_diagonal(jnp.float32)
    total = jnp.zeros((BLOCK, BLOCK), jnp.float32)
    for begin, end in ((0, 5), (5, 9), (9, 13), (13, 17)):
        right = [
            band if u == 0 else block_of(z_all, block_ref[b, u - 1]) for u in range(begin, end)
        ]
        base = 0.5 + lax.dot_general(
            left, jnp.concatenate(right, axis=0), NT, preferred_element_type=jnp.float32
        )
        second = base * base
        fourth = second * second
        soft = fourth * fourth * fourth
        for u in range(begin, end):
            tile = soft[:, (u - begin) * BLOCK : (u - begin + 1) * BLOCK]
            if u == 0:
                tile = tile * apart
            else:
                if u <= OWN:
                    tile = tile * (1.0 - same_ref[b, u - 1] * (1.0 - apart))
                    own_tiles[at, (u - 1) * BLOCK : u * BLOCK] = tile.astype(jnp.bfloat16)
                tile = tile * weight_ref[b, u - 1]
            lead[at, u * BLOCK : (u + 1) * BLOCK] = tile.astype(jnp.bfloat16)
            total = total + tile
    return jnp.sum(jnp.transpose(total), axis=0, keepdims=True)


def fill_pair(b, block_ref, z_all, own_tiles, pair):
    at = pl.ds(pl.multiple_of(b * BLOCK, BLOCK), BLOCK)
    own = [block_of(z_all, block_ref[b, c]) for c in range(OWN)]
    right = jnp.concatenate(own, axis=0) * jnp.bfloat16(0.5)
    apart = off_diagonal(jnp.bfloat16)
    pair[0:BLOCK, :] = own_tiles[at, :]
    for u in range(0, LIST, OWN):
        left = jnp.concatenate([block_of(z_all, block_ref[b, u + i]) for i in range(OWN)], axis=0)
        base = 0.5 + lax.dot_general(left, right, NT, preferred_element_type=jnp.float32)
        second = base * base
        fourth = (second * second).astype(jnp.bfloat16)
        soft = fourth * fourth * fourth
        top = (u + 1) * BLOCK
        pair[top : top + OWN * BLOCK, :] = soft
        if u == 0:
            for c in range(OWN):
                tile = slice(c * BLOCK, (c + 1) * BLOCK)
                pair[top + c * BLOCK : top + (c + 1) * BLOCK, tile] = soft[tile, tile] * apart


def sum_band(b, lead, own_tiles, sums, pair):
    at = pl.ds(pl.multiple_of(b * BLOCK, BLOCK), BLOCK)
    shared = jnp.dot(lead[at, :], pair[...], preferred_element_type=jnp.float32)
    numerator = shared + own_tiles[at, :].astype(jnp.float32)
    for c in range(OWN):
        sums[b, c] = numerator[:, c * BLOCK : (c + 1) * BLOCK]


def divide_band(b, my_degrees, spot_ref, degrees, own_tiles, sums):
    at = pl.ds(pl.multiple_of(b * BLOCK, BLOCK), BLOCK)
    own_row = degrees[pl.ds(my_degrees + b, 1), :]
    own = jnp.transpose(jnp.broadcast_to(own_row, (BLOCK, BLOCK)))
    for c in range(OWN):
        near = degrees[pl.ds(spot_ref[b, c], 1), :]
        link = own_tiles[at, c * BLOCK : (c + 1) * BLOCK].astype(jnp.float32)
        sums[b, c] = sums[b, c] / (jnp.minimum(own, near) + 1.0 - link)


def kernel(
    x_ref, block_ref, weight_ref, same_ref, spot_ref,
    out_ref,
    z_all, lead, own_tiles, sums, degrees, pair, later_pair,
    piece_recv, piece_send, core_recv, core_send, degree_recv, degree_send, out_sem,
):
    row = lax.axis_index("rows")
    plane = lax.axis_index("nbr")
    core, chip = row % 2, row // 2
    y, z = chip % YS, chip // YS
    odd = plane % 2

    def device(to_z, to_y):
        return (((to_z + ZS) % ZS * YS + (to_y + YS) % YS) * 2 + core, plane)

    links = {
        "z+": device(z + 1, y), "z-": device(z - 1, y),
        "y+": device(z, y + 1), "y-": device(z, y - 1),
        "x+": (row, (plane + 1) % XS), "x-": (row, (plane + XS - 1) % XS),
    }
    other = (chip * 2 + 1 - core, plane)
    along_z = {dz: device(z + dz, y) for dz in range(1, ZS)}
    along_y = {dy: device(z, y + dy) for dy in range(1, YS)}
    barrier = pltpu.get_barrier_semaphore()
    greeted = list(along_z.values()) + list(along_y.values()) + [links["x+"], links["x-"], other]
    for neighbour in greeted:
        pl.semaphore_signal(barrier, inc=1, device_id=neighbour, device_id_type=MESH)
    mine = core * HALF + chip * SHARD
    standardize_into(x_ref, z_all, mine)
    pl.semaphore_wait(barrier, len(greeted))

    starts = {
        "A": START["A"],
        "B": START["B"] + odd * (START["C"] - START["B"]),
        "C": START["C"] - odd * (START["C"] - START["B"]),
    }

    def rows_at(kind, part, dy, dz):
        owner = (z - dz + ZS) % ZS * YS + (y - dy + YS) % YS
        rows = piece_rows(kind)
        first = core * HALF + owner * SHARD + starts[kind] + (rows if part == "b" else 0)
        return z_all.at[pl.ds(pl.multiple_of(first, 16), rows)]

    def copy(ref, send, recv, to):
        return pltpu.make_async_remote_copy(
            src_ref=ref, dst_ref=ref, send_sem=send, recv_sem=recv, device_id=to, device_id_type=MESH
        )

    shard = z_all.at[pl.ds(pl.multiple_of(mine, SHARD), SHARD)]
    sent_rows = 0
    for event in PLAN:
        link, kind, part, dy, dz = event
        ref = rows_at(kind, part, dy, dz)
        if link is not None:
            copy(ref, piece_send, piece_recv.at[ARRIVALS[event]], links[link]).wait_recv()
        for send in next_sends(kind, part, dy, dz):
            sent_rows += piece_rows(kind)
            copy(ref, piece_send, piece_recv.at[ARRIVALS[send]], links[send[0]]).start()
        if link is not None:
            copy(ref, core_send, core_recv, other).start()
        elif kind == "A" and part == "b":
            copy(shard, core_send, core_recv, other).start()

    def drain(sem, first, rows):
        ref = z_all.at[pl.ds(first, rows)]
        pltpu.make_async_copy(ref, ref, sem).wait()

    drain(core_recv, pl.multiple_of((1 - core) * HALF, HALF), HALF)

    column = core * (CHIPS * BANDS) + y * (ZS * BANDS)
    my_degrees = column + z * BANDS

    def lead_step(step, carry):
        for i in range(4):
            b = 4 * step + i
            degrees[pl.ds(my_degrees + b, 1), :] = lead_band(
                b, mine // BLOCK, block_ref, weight_ref, same_ref, z_all, lead, own_tiles
            )
        return carry

    lax.fori_loop(0, BANDS // 4, lead_step, 0)

    def of_device(dz):
        return degrees.at[pl.ds(pl.multiple_of(column + (z - dz + ZS) % ZS * BANDS, BANDS), BANDS)]

    def of_column(dy):
        first = core * (CHIPS * BANDS) + (y - dy + YS) % YS * (ZS * BANDS)
        return degrees.at[pl.ds(pl.multiple_of(first, ZS * BANDS), ZS * BANDS)]

    def of_core(which):
        return degrees.at[pl.ds(pl.multiple_of(which * (CHIPS * BANDS), CHIPS * BANDS), CHIPS * BANDS)]

    def passed(number, ref, to):
        return copy(ref, degree_send.at[number], degree_recv.at[number], to)

    def exchange(stage):
        if stage == 1:
            for dz in range(1, ZS):
                passed(dz, of_device(dz), along_z[dz]).wait()
        if stage == 2:
            for dy in range(1, YS):
                passed(ZS + dy, of_column(dy), along_y[dy]).wait()
        if stage == 3:
            passed(0, of_core(1 - core), other).wait()
        if stage == 0:
            for dz in range(1, ZS):
                passed(dz, of_device(0), along_z[dz]).start()
        if stage == 1:
            for dy in range(1, YS):
                passed(ZS + dy, of_column(0), along_y[dy]).start()
        if stage == 2:
            passed(0, of_core(core), other).start()

    fill_pair(0, block_ref, z_all, own_tiles, pair)

    def sum_step(step, carry):
        for stage in range(3):
            pl.when(step == 2 * stage)(lambda stage=stage: exchange(stage))
        b = 2 * step
        fill_pair(b + 1, block_ref, z_all, own_tiles, later_pair)
        sum_band(b, lead, own_tiles, sums, pair)
        fill_pair(b + 2, block_ref, z_all, own_tiles, pair)
        sum_band(b + 1, lead, own_tiles, sums, later_pair)
        return carry

    lax.fori_loop(0, BANDS // 2 - 1, sum_step, 0)
    fill_pair(BANDS - 1, block_ref, z_all, own_tiles, later_pair)
    sum_band(BANDS - 2, lead, own_tiles, sums, pair)
    sum_band(BANDS - 1, lead, own_tiles, sums, later_pair)
    exchange(3)

    def divide_step(step, carry):
        for i in range(2):
            divide_band(2 * step + i, my_degrees, spot_ref, degrees, own_tiles, sums)
        two = pl.ds(2 * step, 2)
        pltpu.make_async_copy(sums.at[two], out_ref.at[two], out_sem).start()
        return carry

    lax.fori_loop(0, BANDS // 2, divide_step, 0)
    pltpu.make_async_copy(sums, out_ref, out_sem).wait()
    drain(piece_send, 0, sent_rows)
    drain(core_send, 0, HALF)


def per_device(expression, nbr_owner, nbr_slot):
    row = lax.axis_index("rows")
    plane = lax.axis_index("nbr")
    owner = lax.dynamic_slice_in_dim(nbr_owner, row * BANDS, BANDS, 1)
    slot = lax.dynamic_slice_in_dim(nbr_slot, row * BANDS, BANDS, 1)

    def own_first(part):
        turned = jnp.stack([lax.dynamic_index_in_dim(part, (plane + i) % XS, 0, False) for i in range(XS)])
        return jnp.transpose(turned, (1, 0, 2)).reshape(BANDS, LIST)

    owner, slot = own_first(owner), own_first(slot)
    core, chip = owner % 2, owner // 2
    block = core * (CHIPS * BANDS) + chip * BANDS + slot
    ids = owner * BANDS + slot
    same = ids == (row * BANDS + jnp.arange(BANDS, dtype=jnp.int32))[:, None]
    position = jnp.arange(LIST, dtype=jnp.int32)
    earlier = position[None, :] < position[:, None]
    repeated = jnp.any((ids[:, :, None] == ids[:, None, :]) & earlier[None], axis=2)
    weights = (~same & ~repeated).astype(jnp.float32)
    spot = core * (CHIPS * BANDS) + (chip % YS) * (ZS * BANDS) + chip // YS * BANDS + slot
    return pl.pallas_call(
        kernel,
        out_shape=jax.ShapeDtypeStruct((BANDS, OWN, BLOCK, BLOCK), jnp.float32),
        in_specs=[pl.BlockSpec(memory_space=pltpu.VMEM)]
        + [pl.BlockSpec(memory_space=pltpu.SMEM)] * 4,
        out_specs=pl.BlockSpec(memory_space=pl.ANY),
        scratch_shapes=[
            pltpu.VMEM((2 * HALF, BLOCK), jnp.bfloat16),
            pltpu.VMEM((SHARD, WIDTH), jnp.bfloat16),
            pltpu.VMEM((SHARD, OWN_WIDTH), jnp.bfloat16),
            pltpu.VMEM((BANDS, OWN, BLOCK, BLOCK), jnp.float32),
            pltpu.VMEM((2 * CHIPS * BANDS, BLOCK), jnp.float32),
            pltpu.VMEM((WIDTH, OWN_WIDTH), jnp.bfloat16),
            pltpu.VMEM((WIDTH, OWN_WIDTH), jnp.bfloat16),
            pltpu.SemaphoreType.DMA((len(PLAN),)),
            pltpu.SemaphoreType.DMA,
            pltpu.SemaphoreType.DMA,
            pltpu.SemaphoreType.DMA,
            pltpu.SemaphoreType.DMA((ZS + YS,)),
            pltpu.SemaphoreType.DMA((ZS + YS,)),
            pltpu.SemaphoreType.DMA,
        ],
        compiler_params=pltpu.CompilerParams(
            collective_id=0, has_side_effects=True, vmem_limit_bytes=60 * 2**20
        ),
    )(expression, block, weights, same[:, :OWN].astype(jnp.float32), spot[:, :OWN])


def solution(mesh):
    return jax.shard_map(
        per_device,
        mesh=mesh,
        in_specs=(P("rows", None, None), P(), P()),
        out_specs=P("rows", "nbr", None, None),
        check_vma=False,
    )
```

```python
import heapq

import jax
import jax.numpy as jnp
from jax import lax
from jax.experimental import pallas as pl
from jax.experimental.pallas import tpu as pltpu
from jax.sharding import PartitionSpec as P

MESH = pl.DeviceIdType.MESH
BLOCK = 128
BANDS = 16
LIST = 16
OWN = 4
ZS, YS, XS = 8, 4, 4
CHIPS = ZS * YS
SHARD = BANDS * BLOCK
HALF = CHIPS * SHARD
ROWS = {("A", "a"): 272, ("A", "b"): 272, ("B", "a"): 416, ("B", "b"): 416, ("C", "a"): 416, ("C", "b"): 256}
EVEN = {("A", "a"): 0, ("A", "b"): 272, ("B", "a"): 544, ("B", "b"): 960, ("C", "a"): 544, ("C", "b"): 960}
ODD = {("A", "a"): 0, ("A", "b"): 272, ("B", "a"): 1632, ("B", "b"): 1216, ("C", "a"): 1632, ("C", "b"): 1376}
WIDTH = LIST * BLOCK + BLOCK
OWN_WIDTH = OWN * BLOCK
NT = (((1,), (1,)), ((), ()))


def next_sends(kind, part, dy, dz):
    sends = []
    if kind == "C":
        return sends
    along_z, along_y = [], []
    if 0 <= dz < 3:
        along_z.append(("z+", kind, part, dy, dz + 1))
    if dz == 3 and part == "a":
        along_z.append(("z+", kind, part, dy, 4))
    if -3 < dz <= 0:
        along_z.append(("z-", kind, part, dy, dz - 1))
    if dz == -3 and part == "b":
        along_z.append(("z-", kind, part, dy, -4))
    if dy == 0:
        along_y += [("y+", kind, part, 1, dz), ("y-", kind, part, -1, dz)]
    if dy == 1 and part == "a":
        along_y.append(("y+", kind, part, 2, dz))
    if dy == -1 and part == "b":
        along_y.append(("y-", kind, part, -2, dz))
    if kind == "A":
        sends += along_y if dz == 0 else []
        sends += along_z
    else:
        sends += along_z if dy == 0 else []
        sends += along_y
        if dy or dz:
            sends.append(("x+" if dz % 2 == 0 else "x-", "C", part, dy, dz))
    return sends


def gather_plan():
    free, heap, order, count, clock = {}, [], [], 0, 0.0
    for kind, part in (("B", "a"), ("B", "b"), ("A", "a"), ("A", "b")):
        heapq.heappush(heap, (0.0, count, (None, kind, part, 0, 0)))
        count += 1
    while heap:
        time, _, event = heapq.heappop(heap)
        order.append(event)
        clock = max(clock, time) + 0.1
        for send in next_sends(*event[1:]):
            began = max(free.get(send[0], 0.0), clock)
            free[send[0]] = began + 2 * ROWS[send[1:3]] * 256 / 95e3
            heapq.heappush(heap, (free[send[0]] + 3.2, count, send))
            count += 1
    return order


PLAN = gather_plan()
ARRIVALS = {event: number for number, event in enumerate(PLAN)}


def standardize_into(x_ref, z_all, mine):
    def four(step, carry):
        for i in range(4):
            block = 4 * step + i
            values = x_ref[block].astype(jnp.float32)
            centred = values - jnp.mean(values, axis=-1, keepdims=True)
            inverse = lax.rsqrt(jnp.sum(centred * centred, axis=-1, keepdims=True) + 1e-06)
            rows = pl.ds(pl.multiple_of(mine + block * BLOCK, BLOCK), BLOCK)
            z_all[rows, :] = (centred * inverse).astype(jnp.bfloat16)
        return carry

    lax.fori_loop(0, BANDS // 4, four, 0)


def list_blocks(row, plane, lists, blocks, weights):
    groups = [(plane + i) % XS for i in range(XS)]
    owner = jnp.concatenate([lists[0, group] for group in groups], axis=0)
    slot = jnp.concatenate([lists[1, group] for group in groups], axis=0)
    block = (owner & 1) * (CHIPS * BANDS) + (owner >> 1) * BANDS + slot
    lane = lax.broadcasted_iota(jnp.int32, (LIST, BLOCK), 1)
    place = lax.broadcasted_iota(jnp.int32, (LIST, BLOCK), 0)
    band_row = row // 8 * 8 + (lane >> 4)
    band = (band_row & 1) * (CHIPS * BANDS) + (band_row >> 1) * BANDS + (lane & 15)
    kept = jnp.where(block == band, 0.0, 1.0)
    for earlier in range(LIST - 1):
        repeats = (block == block[earlier : earlier + 1]) & (place > earlier)
        kept = jnp.where(repeats, 0.0, kept)
    blocks[...] = block
    weights[...] = kept


def off_diagonal(dtype):
    i = lax.broadcasted_iota(jnp.int32, (BLOCK, BLOCK), 0)
    j = lax.broadcasted_iota(jnp.int32, (BLOCK, BLOCK), 1)
    return jnp.where(i == j, 0.0, 1.0).astype(dtype)


def block_of(z_all, block):
    return z_all[pl.ds(block * BLOCK, BLOCK), :]


def lead_band(b, my_block, listed, weight, z_all, lead, own_tiles):
    band = block_of(z_all, my_block + b)
    left = band * jnp.bfloat16(0.5)
    at = pl.ds(pl.multiple_of(b * BLOCK, BLOCK), BLOCK)
    apart = off_diagonal(jnp.float32)
    total = jnp.zeros((BLOCK, BLOCK), jnp.float32)
    for begin, end in ((0, 5), (5, 9), (9, 13), (13, 17)):
        right = [
            band if u == 0 else block_of(z_all, listed(b, u - 1)) for u in range(begin, end)
        ]
        base = 0.5 + lax.dot_general(
            left, jnp.concatenate(right, axis=0), NT, preferred_element_type=jnp.float32
        )
        second = base * base
        fourth = second * second
        soft = fourth * fourth * fourth
        for u in range(begin, end):
            tile = soft[:, (u - begin) * BLOCK : (u - begin + 1) * BLOCK]
            if u == 0:
                tile = tile * apart
            else:
                if u <= OWN:
                    tile = tile * (1.0 - (1.0 - weight(b, u - 1)) * (1.0 - apart))
                    own_tiles[at, (u - 1) * BLOCK : u * BLOCK] = tile.astype(jnp.bfloat16)
                tile = tile * weight(b, u - 1)
            lead[at, u * BLOCK : (u + 1) * BLOCK] = tile.astype(jnp.bfloat16)
            total = total + tile
    return jnp.sum(jnp.transpose(total), axis=0, keepdims=True)


def fill_pair(b, listed, z_all, own_tiles, pair):
    at = pl.ds(pl.multiple_of(b * BLOCK, BLOCK), BLOCK)
    own = [block_of(z_all, listed(b, c)) for c in range(OWN)]
    right = jnp.concatenate(own, axis=0) * jnp.bfloat16(0.5)
    apart = off_diagonal(jnp.bfloat16)
    pair[0:BLOCK, :] = own_tiles[at, :]
    for u in range(0, LIST, OWN):
        left = jnp.concatenate([block_of(z_all, listed(b, u + i)) for i in range(OWN)], axis=0)
        base = 0.5 + lax.dot_general(left, right, NT, preferred_element_type=jnp.float32)
        second = base * base
        fourth = (second * second).astype(jnp.bfloat16)
        soft = fourth * fourth * fourth
        top = (u + 1) * BLOCK
        pair[top : top + OWN * BLOCK, :] = soft
        if u == 0:
            for c in range(OWN):
                tile = slice(c * BLOCK, (c + 1) * BLOCK)
                pair[top + c * BLOCK : top + (c + 1) * BLOCK, tile] = soft[tile, tile] * apart


def sum_band(b, lead, own_tiles, sums, pair):
    at = pl.ds(pl.multiple_of(b * BLOCK, BLOCK), BLOCK)
    shared = jnp.dot(lead[at, :], pair[...], preferred_element_type=jnp.float32)
    numerator = shared + own_tiles[at, :].astype(jnp.float32)
    for c in range(OWN):
        sums[b, c] = numerator[:, c * BLOCK : (c + 1) * BLOCK]


def divide_band(b, my_degrees, listed, degrees, own_tiles, sums):
    at = pl.ds(pl.multiple_of(b * BLOCK, BLOCK), BLOCK)
    own_row = degrees[pl.ds(my_degrees + b, 1), :]
    own = jnp.transpose(jnp.broadcast_to(own_row, (BLOCK, BLOCK)))
    for c in range(OWN):
        near = degrees[pl.ds(listed(b, c), 1), :]
        link = own_tiles[at, c * BLOCK : (c + 1) * BLOCK].astype(jnp.float32)
        sums[b, c] = sums[b, c] / (jnp.minimum(own, near) + 1.0 - link)


def kernel(
    x_ref, owner_ref, slot_ref,
    out_ref,
    lists, blocks, weights, block_ref, weight_ref,
    z_all, lead, own_tiles, sums, degrees, pair, later_pair,
    piece_recv, piece_send, core_recv, core_send, degree_recv, degree_send, out_sem, list_sem,
):
    row = lax.axis_index("rows")
    plane = lax.axis_index("nbr")
    core, chip = row % 2, row // 2
    y, z = chip % YS, chip // YS
    odd = plane % 2

    def device(to_z, to_y):
        return (((to_z + ZS) % ZS * YS + (to_y + YS) % YS) * 2 + core, plane)

    links = {
        "z+": device(z + 1, y), "z-": device(z - 1, y),
        "y+": device(z, y + 1), "y-": device(z, y - 1),
        "x+": (row, (plane + 1) % XS), "x-": (row, (plane + XS - 1) % XS),
    }
    other = (chip * 2 + 1 - core, plane)
    along_z = {dz: device(z + dz, y) for dz in range(1, ZS)}
    along_y = {dy: device(z, y + dy) for dy in range(1, YS)}
    barrier = pltpu.get_barrier_semaphore()
    greeted = list(along_z.values()) + list(along_y.values()) + [links["x+"], links["x-"], other]
    for neighbour in greeted:
        pl.semaphore_signal(barrier, inc=1, device_id=neighbour, device_id_type=MESH)
    window = pl.ds(pl.multiple_of(row // 8 * BLOCK, BLOCK), BLOCK)
    list_copies = [
        pltpu.make_async_copy(ref.at[:, :, window], lists.at[i], list_sem.at[i])
        for i, ref in enumerate((owner_ref, slot_ref))
    ]
    for list_copy in list_copies:
        list_copy.start()
    mine = core * HALF + chip * SHARD
    standardize_into(x_ref, z_all, mine)
    pl.semaphore_wait(barrier, len(greeted))

    def rows_at(kind, part, dy, dz, parity):
        owner = (z - dz + ZS) % ZS * YS + (y - dy + YS) % YS
        first = core * HALF + owner * SHARD + EVEN[kind, part]
        apart = ODD[kind, part] - EVEN[kind, part]
        if apart:
            first = first + parity * apart
        return z_all.at[pl.ds(pl.multiple_of(first, 16), ROWS[kind, part])]

    def copy(ref, send, recv, to):
        return pltpu.make_async_remote_copy(
            src_ref=ref, dst_ref=ref, send_sem=send, recv_sem=recv, device_id=to, device_id_type=MESH
        )

    shard = z_all.at[pl.ds(pl.multiple_of(mine, SHARD), SHARD)]
    sent_rows = 0
    for number, event in enumerate(PLAN):
        link, kind, part, dy, dz = event
        ref = rows_at(kind, part, dy, dz, 1 - odd if kind == "C" else odd)
        if number == 4:
            for list_copy in list_copies:
                list_copy.wait()
            list_blocks(row, plane, lists, blocks, weights)
            number_copies = [
                pltpu.make_async_copy(blocks, block_ref, list_sem.at[0]),
                pltpu.make_async_copy(weights, weight_ref, list_sem.at[1]),
            ]
            for number_copy in number_copies:
                number_copy.start()
        if link is not None:
            copy(ref, piece_send, piece_recv.at[ARRIVALS[event]], links[link]).wait_recv()
        for send in next_sends(kind, part, dy, dz):
            sent_rows += ROWS[send[1:3]]
            sent = rows_at("C", part, dy, dz, odd) if send[1] == "C" else ref
            copy(sent, piece_send, piece_recv.at[ARRIVALS[send]], links[send[0]]).start()
        if link is not None:
            copy(ref, core_send, core_recv, other).start()
        elif kind == "A" and part == "b":
            copy(shard, core_send, core_recv, other).start()
    for number_copy in number_copies:
        number_copy.wait()
    first_lane = row % 8 * BANDS

    def listed(b, k):
        return block_ref[k, first_lane + b]

    def weight(b, k):
        return weight_ref[k, first_lane + b]

    def drain(sem, first, rows):
        ref = z_all.at[pl.ds(first, rows)]
        pltpu.make_async_copy(ref, ref, sem).wait()

    drain(core_recv, pl.multiple_of((1 - core) * HALF, HALF), HALF)

    my_degrees = mine // BLOCK

    def lead_step(step, carry):
        for i in range(4):
            b = 4 * step + i
            degrees[pl.ds(my_degrees + b, 1), :] = lead_band(
                b, mine // BLOCK, listed, weight, z_all, lead, own_tiles
            )
        return carry

    lax.fori_loop(0, BANDS // 4, lead_step, 0)

    def of_device(dy):
        first = core * (CHIPS * BANDS) + (z * YS + (y - dy + YS) % YS) * BANDS
        return degrees.at[pl.ds(pl.multiple_of(first, BANDS), BANDS)]

    def of_line(dz):
        first = core * (CHIPS * BANDS) + (z - dz + ZS) % ZS * (YS * BANDS)
        return degrees.at[pl.ds(pl.multiple_of(first, YS * BANDS), YS * BANDS)]

    def of_core(which):
        return degrees.at[pl.ds(pl.multiple_of(which * (CHIPS * BANDS), CHIPS * BANDS), CHIPS * BANDS)]

    def passed(number, ref, to):
        return copy(ref, degree_send.at[number], degree_recv.at[number], to)

    def exchange(stage):
        if stage == 1:
            for dy in range(1, YS):
                passed(ZS + dy, of_device(dy), along_y[dy]).wait()
        if stage == 2:
            for dz in range(1, ZS):
                passed(dz, of_line(dz), along_z[dz]).wait()
        if stage == 3:
            passed(0, of_core(1 - core), other).wait()
        if stage == 0:
            for dy in range(1, YS):
                passed(ZS + dy, of_device(0), along_y[dy]).start()
        if stage == 1:
            for dz in range(1, ZS):
                passed(dz, of_line(0), along_z[dz]).start()
        if stage == 2:
            passed(0, of_core(core), other).start()

    fill_pair(0, listed, z_all, own_tiles, pair)

    def sum_step(step, carry):
        for stage in range(3):
            pl.when(step == 2 * stage)(lambda stage=stage: exchange(stage))
        b = 2 * step
        fill_pair(b + 1, listed, z_all, own_tiles, later_pair)
        sum_band(b, lead, own_tiles, sums, pair)
        fill_pair(b + 2, listed, z_all, own_tiles, pair)
        sum_band(b + 1, lead, own_tiles, sums, later_pair)
        return carry

    lax.fori_loop(0, BANDS // 2 - 1, sum_step, 0)
    fill_pair(BANDS - 1, listed, z_all, own_tiles, later_pair)
    sum_band(BANDS - 2, lead, own_tiles, sums, pair)
    sum_band(BANDS - 1, lead, own_tiles, sums, later_pair)
    exchange(3)

    def divide_step(step, carry):
        for i in range(2):
            divide_band(2 * step + i, my_degrees, listed, degrees, own_tiles, sums)
        two = pl.ds(2 * step, 2)
        pltpu.make_async_copy(sums.at[two], out_ref.at[two], out_sem).start()
        return carry

    lax.fori_loop(0, BANDS // 2, divide_step, 0)
    pltpu.make_async_copy(sums, out_ref, out_sem).wait()
    drain(piece_send, 0, sent_rows)
    drain(core_send, 0, HALF)


def per_device(expression, nbr_owner, nbr_slot):
    return pl.pallas_call(
        kernel,
        out_shape=jax.ShapeDtypeStruct((BANDS, OWN, BLOCK, BLOCK), jnp.float32),
        in_specs=[pl.BlockSpec(memory_space=pltpu.VMEM)]
        + [pl.BlockSpec(memory_space=pl.ANY)] * 2,
        out_specs=pl.BlockSpec(memory_space=pl.ANY),
        scratch_shapes=[
            pltpu.VMEM((2, XS, OWN, BLOCK), jnp.int32),
            pltpu.VMEM((LIST, BLOCK), jnp.int32),
            pltpu.VMEM((LIST, BLOCK), jnp.float32),
            pltpu.SMEM((LIST, BLOCK), jnp.int32),
            pltpu.SMEM((LIST, BLOCK), jnp.float32),
            pltpu.VMEM((2 * HALF, BLOCK), jnp.bfloat16),
            pltpu.VMEM((SHARD, WIDTH), jnp.bfloat16),
            pltpu.VMEM((SHARD, OWN_WIDTH), jnp.bfloat16),
            pltpu.VMEM((BANDS, OWN, BLOCK, BLOCK), jnp.float32),
            pltpu.VMEM((2 * CHIPS * BANDS, BLOCK), jnp.float32),
            pltpu.VMEM((WIDTH, OWN_WIDTH), jnp.bfloat16),
            pltpu.VMEM((WIDTH, OWN_WIDTH), jnp.bfloat16),
            pltpu.SemaphoreType.DMA((len(PLAN),)),
            pltpu.SemaphoreType.DMA,
            pltpu.SemaphoreType.DMA,
            pltpu.SemaphoreType.DMA,
            pltpu.SemaphoreType.DMA((ZS + YS,)),
            pltpu.SemaphoreType.DMA((ZS + YS,)),
            pltpu.SemaphoreType.DMA,
            pltpu.SemaphoreType.DMA((2,)),
        ],
        compiler_params=pltpu.CompilerParams(
            collective_id=0, has_side_effects=True, vmem_limit_bytes=60 * 2**20
        ),
    )(expression, jnp.transpose(nbr_owner, (0, 2, 1)), jnp.transpose(nbr_slot, (0, 2, 1)))


def solution(mesh):
    return jax.shard_map(
        per_device,
        mesh=mesh,
        in_specs=(P("rows", None, None), P(), P()),
        out_specs=P("rows", "nbr", None, None),
        check_vma=False,
    )
```

```python
import heapq

import jax
import jax.numpy as jnp
from jax import lax
from jax.experimental import pallas as pl
from jax.experimental.pallas import tpu as pltpu
from jax.sharding import PartitionSpec as P

MESH = pl.DeviceIdType.MESH
BLOCK = 128
BANDS = 16
LIST = 16
OWN = 4
ZS, YS, XS = 8, 4, 4
CHIPS = ZS * YS
SHARD = BANDS * BLOCK
HALF = CHIPS * SHARD
ROWS = {("A", "a"): 320, ("A", "b"): 320, ("B", "a"): 368, ("B", "b"): 368, ("C", "a"): 368, ("C", "b"): 304}
EVEN = {("A", "a"): 0, ("A", "b"): 320, ("B", "a"): 640, ("B", "b"): 1008, ("C", "a"): 640, ("C", "b"): 1008}
ODD = {("A", "a"): 0, ("A", "b"): 320, ("B", "a"): 1680, ("B", "b"): 1312, ("C", "a"): 1680, ("C", "b"): 1376}
WIDTH = LIST * BLOCK + BLOCK
OWN_WIDTH = OWN * BLOCK
NT = (((1,), (1,)), ((), ()))


def next_sends(kind, part, dy, dz):
    sends = []
    if kind == "C":
        return sends
    along_z, along_y = [], []
    if 0 <= dz < 3:
        along_z.append(("z+", kind, part, dy, dz + 1))
    if dz == 3 and part == "a":
        along_z.append(("z+", kind, part, dy, 4))
    if -3 < dz <= 0:
        along_z.append(("z-", kind, part, dy, dz - 1))
    if dz == -3 and part == "b":
        along_z.append(("z-", kind, part, dy, -4))
    if dy == 0:
        along_y += [("y+", kind, part, 1, dz), ("y-", kind, part, -1, dz)]
    if dy == 1 and part == "a":
        along_y.append(("y+", kind, part, 2, dz))
    if dy == -1 and part == "b":
        along_y.append(("y-", kind, part, -2, dz))
    if kind == "A":
        sends += along_y if dz == 0 else []
        sends += along_z
    else:
        sends += along_z if dy == 0 else []
        sends += along_y
        if dy or dz:
            sends.append(("x+" if dz % 2 == 0 else "x-", "C", part, dy, dz))
    return sends


def gather_plan():
    free, heap, order, count, clock = {}, [], [], 0, 0.0
    for kind, part in (("B", "a"), ("B", "b"), ("A", "a"), ("A", "b")):
        heapq.heappush(heap, (0.0, count, (None, kind, part, 0, 0)))
        count += 1
    while heap:
        time, _, event = heapq.heappop(heap)
        order.append(event)
        clock = max(clock, time) + 0.1
        for send in next_sends(*event[1:]):
            began = max(free.get(send[0], 0.0), clock)
            free[send[0]] = began + 2 * ROWS[send[1:3]] * 256 / 95e3
            heapq.heappush(heap, (free[send[0]] + 3.2, count, send))
            count += 1
    return order


PLAN = gather_plan()
ARRIVALS = {event: number for number, event in enumerate(PLAN)}


def standardize_into(x_ref, z_all, mine):
    def four(step, carry):
        for i in range(4):
            block = 4 * step + i
            values = x_ref[block].astype(jnp.float32)
            centred = values - jnp.mean(values, axis=-1, keepdims=True)
            inverse = lax.rsqrt(jnp.sum(centred * centred, axis=-1, keepdims=True) + 1e-06)
            rows = pl.ds(pl.multiple_of(mine + block * BLOCK, BLOCK), BLOCK)
            z_all[rows, :] = (centred * inverse).astype(jnp.bfloat16)
        return carry

    lax.fori_loop(0, BANDS // 4, four, 0)


def list_blocks(row, plane, lists, blocks, weights):
    groups = [(plane + i) % XS for i in range(XS)]
    owner = jnp.concatenate([lists[0, group] for group in groups], axis=0)
    slot = jnp.concatenate([lists[1, group] for group in groups], axis=0)
    block = (owner & 1) * (CHIPS * BANDS) + (owner >> 1) * BANDS + slot
    lane = lax.broadcasted_iota(jnp.int32, (LIST, BLOCK), 1)
    place = lax.broadcasted_iota(jnp.int32, (LIST, BLOCK), 0)
    band_row = row // 8 * 8 + (lane >> 4)
    band = (band_row & 1) * (CHIPS * BANDS) + (band_row >> 1) * BANDS + (lane & 15)
    kept = jnp.where(block == band, 0.0, 1.0)
    for earlier in range(LIST - 1):
        repeats = (block == block[earlier : earlier + 1]) & (place > earlier)
        kept = jnp.where(repeats, 0.0, kept)
    blocks[...] = block
    weights[...] = kept


def off_diagonal(dtype):
    i = lax.broadcasted_iota(jnp.int32, (BLOCK, BLOCK), 0)
    j = lax.broadcasted_iota(jnp.int32, (BLOCK, BLOCK), 1)
    return jnp.where(i == j, 0.0, 1.0).astype(dtype)


def block_of(z_all, block):
    return z_all[pl.ds(block * BLOCK, BLOCK), :]


def lead_band(b, my_block, listed, weight, z_all, lead, own_tiles):
    band = block_of(z_all, my_block + b)
    left = band * jnp.bfloat16(0.5)
    at = pl.ds(pl.multiple_of(b * BLOCK, BLOCK), BLOCK)
    apart = off_diagonal(jnp.float32)
    total = jnp.zeros((BLOCK, BLOCK), jnp.float32)
    for begin, end in ((0, 5), (5, 9), (9, 13), (13, 17)):
        right = [
            band if u == 0 else block_of(z_all, listed(b, u - 1)) for u in range(begin, end)
        ]
        base = 0.5 + lax.dot_general(
            left, jnp.concatenate(right, axis=0), NT, preferred_element_type=jnp.float32
        )
        second = base * base
        fourth = second * second
        soft = fourth * fourth * fourth
        for u in range(begin, end):
            tile = soft[:, (u - begin) * BLOCK : (u - begin + 1) * BLOCK]
            if u == 0:
                tile = tile * apart
            else:
                if u <= OWN:
                    tile = tile * (1.0 - (1.0 - weight(b, u - 1)) * (1.0 - apart))
                    own_tiles[at, (u - 1) * BLOCK : u * BLOCK] = tile.astype(jnp.bfloat16)
                tile = tile * weight(b, u - 1)
            lead[at, u * BLOCK : (u + 1) * BLOCK] = tile.astype(jnp.bfloat16)
            total = total + tile
    return jnp.sum(jnp.transpose(total), axis=0, keepdims=True)


def fill_pair(b, listed, z_all, own_tiles, pair):
    at = pl.ds(pl.multiple_of(b * BLOCK, BLOCK), BLOCK)
    own = [block_of(z_all, listed(b, c)) for c in range(OWN)]
    right = jnp.concatenate(own, axis=0) * jnp.bfloat16(0.5)
    apart = off_diagonal(jnp.bfloat16)
    pair[0:BLOCK, :] = own_tiles[at, :]
    for u in range(0, LIST, OWN):
        left = jnp.concatenate([block_of(z_all, listed(b, u + i)) for i in range(OWN)], axis=0)
        base = 0.5 + lax.dot_general(left, right, NT, preferred_element_type=jnp.float32)
        second = base * base
        fourth = (second * second).astype(jnp.bfloat16)
        soft = fourth * fourth * fourth
        top = (u + 1) * BLOCK
        pair[top : top + OWN * BLOCK, :] = soft
        if u == 0:
            for c in range(OWN):
                tile = slice(c * BLOCK, (c + 1) * BLOCK)
                pair[top + c * BLOCK : top + (c + 1) * BLOCK, tile] = soft[tile, tile] * apart


def sum_band(b, lead, own_tiles, sums, pair):
    at = pl.ds(pl.multiple_of(b * BLOCK, BLOCK), BLOCK)
    shared = jnp.dot(lead[at, :], pair[...], preferred_element_type=jnp.float32)
    numerator = shared + own_tiles[at, :].astype(jnp.float32)
    for c in range(OWN):
        sums[b, c] = numerator[:, c * BLOCK : (c + 1) * BLOCK]


def divide(sum_ref, link_ref, own_ref, near_ref, out_ref):
    for b in range(sum_ref.shape[0]):
        own = jnp.transpose(jnp.broadcast_to(own_ref[b : b + 1, :], (BLOCK, BLOCK)))
        for c in range(OWN):
            tile = link_ref[b * BLOCK : (b + 1) * BLOCK, c * BLOCK : (c + 1) * BLOCK]
            link = tile.astype(jnp.float32)
            out_ref[b, c] = sum_ref[b, c] / (jnp.minimum(own, near_ref[b, c : c + 1, :]) + 1.0 - link)


def kernel(
    x_ref, owner_ref, slot_ref,
    sum_out, link_out, own_out, near_out,
    lists, blocks, weights, block_ref, weight_ref,
    z_all, lead, own_tiles, sums, degrees, pair, later_pair,
    piece_recv, piece_send, core_recv, core_send, degree_recv, degree_send, out_sem, list_sem,
):
    row = lax.axis_index("rows")
    plane = lax.axis_index("nbr")
    core, chip = row % 2, row // 2
    y, z = chip % YS, chip // YS
    odd = plane % 2

    def device(to_z, to_y):
        return (((to_z + ZS) % ZS * YS + (to_y + YS) % YS) * 2 + core, plane)

    links = {
        "z+": device(z + 1, y), "z-": device(z - 1, y),
        "y+": device(z, y + 1), "y-": device(z, y - 1),
        "x+": (row, (plane + 1) % XS), "x-": (row, (plane + XS - 1) % XS),
    }
    other = (chip * 2 + 1 - core, plane)
    along_z = {dz: device(z + dz, y) for dz in range(1, ZS)}
    along_y = {dy: device(z, y + dy) for dy in range(1, YS)}
    barrier = pltpu.get_barrier_semaphore()
    greeted = list(along_z.values()) + list(along_y.values()) + [links["x+"], links["x-"], other]
    for neighbour in greeted:
        pl.semaphore_signal(barrier, inc=1, device_id=neighbour, device_id_type=MESH)
    window = pl.ds(pl.multiple_of(row // 8 * BLOCK, BLOCK), BLOCK)
    list_copies = [
        pltpu.make_async_copy(ref.at[:, :, window], lists.at[i], list_sem.at[i])
        for i, ref in enumerate((owner_ref, slot_ref))
    ]
    for list_copy in list_copies:
        list_copy.start()
    mine = core * HALF + chip * SHARD
    standardize_into(x_ref, z_all, mine)
    pl.semaphore_wait(barrier, len(greeted))

    def rows_at(kind, part, dy, dz, parity):
        owner = (z - dz + ZS) % ZS * YS + (y - dy + YS) % YS
        first = core * HALF + owner * SHARD + EVEN[kind, part]
        apart = ODD[kind, part] - EVEN[kind, part]
        if apart:
            first = first + parity * apart
        return z_all.at[pl.ds(pl.multiple_of(first, 16), ROWS[kind, part])]

    def copy(ref, send, recv, to):
        return pltpu.make_async_remote_copy(
            src_ref=ref, dst_ref=ref, send_sem=send, recv_sem=recv, device_id=to, device_id_type=MESH
        )

    shard = z_all.at[pl.ds(pl.multiple_of(mine, SHARD), SHARD)]
    sent_rows = 0
    for number, event in enumerate(PLAN):
        link, kind, part, dy, dz = event
        ref = rows_at(kind, part, dy, dz, 1 - odd if kind == "C" else odd)
        if number == 4:
            for list_copy in list_copies:
                list_copy.wait()
            list_blocks(row, plane, lists, blocks, weights)
            number_copies = [
                pltpu.make_async_copy(blocks, block_ref, list_sem.at[0]),
                pltpu.make_async_copy(weights, weight_ref, list_sem.at[1]),
            ]
            for number_copy in number_copies:
                number_copy.start()
        if link is not None:
            copy(ref, piece_send, piece_recv.at[ARRIVALS[event]], links[link]).wait_recv()
        for send in next_sends(kind, part, dy, dz):
            sent_rows += ROWS[send[1:3]]
            sent = rows_at("C", part, dy, dz, odd) if send[1] == "C" else ref
            copy(sent, piece_send, piece_recv.at[ARRIVALS[send]], links[send[0]]).start()
        if link is not None:
            copy(ref, core_send, core_recv, other).start()
        elif kind == "A" and part == "b":
            copy(shard, core_send, core_recv, other).start()
    for number_copy in number_copies:
        number_copy.wait()
    first_lane = row % 8 * BANDS

    def listed(b, k):
        return block_ref[k, first_lane + b]

    def weight(b, k):
        return weight_ref[k, first_lane + b]

    def drain(sem, first, rows):
        ref = z_all.at[pl.ds(first, rows)]
        pltpu.make_async_copy(ref, ref, sem).wait()

    drain(core_recv, pl.multiple_of((1 - core) * HALF, HALF), HALF)

    my_degrees = mine // BLOCK

    def lead_step(step, carry):
        for i in range(4):
            b = 4 * step + i
            degrees[pl.ds(my_degrees + b, 1), :] = lead_band(
                b, mine // BLOCK, listed, weight, z_all, lead, own_tiles
            )
        return carry

    lax.fori_loop(0, BANDS // 4, lead_step, 0)
    link_copy = pltpu.make_async_copy(own_tiles, link_out, out_sem.at[1])
    link_copy.start()

    def emit(b):
        pltpu.make_async_copy(sums.at[b], sum_out.at[b], out_sem.at[0]).start()

    def of_device(dy):
        first = core * (CHIPS * BANDS) + (z * YS + (y - dy + YS) % YS) * BANDS
        return degrees.at[pl.ds(pl.multiple_of(first, BANDS), BANDS)]

    def of_line(dz):
        first = core * (CHIPS * BANDS) + (z - dz + ZS) % ZS * (YS * BANDS)
        return degrees.at[pl.ds(pl.multiple_of(first, YS * BANDS), YS * BANDS)]

    def of_core(which):
        return degrees.at[pl.ds(pl.multiple_of(which * (CHIPS * BANDS), CHIPS * BANDS), CHIPS * BANDS)]

    def passed(number, ref, to):
        return copy(ref, degree_send.at[number], degree_recv.at[number], to)

    def exchange(stage):
        if stage == 1:
            for dy in range(1, YS):
                passed(ZS + dy, of_device(dy), along_y[dy]).wait()
        if stage == 2:
            for dz in range(1, ZS):
                passed(dz, of_line(dz), along_z[dz]).wait()
        if stage == 3:
            passed(0, of_core(1 - core), other).wait()
        if stage == 0:
            for dy in range(1, YS):
                passed(ZS + dy, of_device(0), along_y[dy]).start()
        if stage == 1:
            for dz in range(1, ZS):
                passed(dz, of_line(0), along_z[dz]).start()
        if stage == 2:
            passed(0, of_core(core), other).start()

    fill_pair(0, listed, z_all, own_tiles, pair)

    def sum_step(step, carry):
        for stage in range(3):
            pl.when(step == 2 * stage)(lambda stage=stage: exchange(stage))
        b = 2 * step
        fill_pair(b + 1, listed, z_all, own_tiles, later_pair)
        sum_band(b, lead, own_tiles, sums, pair)
        fill_pair(b + 2, listed, z_all, own_tiles, pair)
        sum_band(b + 1, lead, own_tiles, sums, later_pair)
        emit(b)
        emit(b + 1)
        return carry

    lax.fori_loop(0, BANDS // 2 - 1, sum_step, 0)
    fill_pair(BANDS - 1, listed, z_all, own_tiles, later_pair)
    sum_band(BANDS - 2, lead, own_tiles, sums, pair)
    sum_band(BANDS - 1, lead, own_tiles, sums, later_pair)
    emit(BANDS - 2)
    emit(BANDS - 1)
    exchange(3)
    own_out[...] = degrees[pl.ds(pl.multiple_of(my_degrees, BANDS), BANDS), :]

    def near_step(b, carry):
        for c in range(OWN):
            near_out[b, c : c + 1, :] = degrees[pl.ds(listed(b, c), 1), :]
        return carry

    lax.fori_loop(0, BANDS, near_step, 0)
    link_copy.wait()
    pltpu.make_async_copy(sums, sum_out, out_sem.at[0]).wait()
    drain(piece_send, 0, sent_rows)
    drain(core_send, 0, HALF)


def per_device(expression, nbr_owner, nbr_slot):
    sums, links, own, near = pl.pallas_call(
        kernel,
        out_shape=(
            jax.ShapeDtypeStruct((BANDS, OWN, BLOCK, BLOCK), jnp.float32),
            jax.ShapeDtypeStruct((SHARD, OWN_WIDTH), jnp.bfloat16),
            jax.ShapeDtypeStruct((BANDS, BLOCK), jnp.float32),
            jax.ShapeDtypeStruct((BANDS, OWN, BLOCK), jnp.float32),
        ),
        in_specs=[pl.BlockSpec(memory_space=pltpu.VMEM)]
        + [pl.BlockSpec(memory_space=pl.ANY)] * 2,
        out_specs=(pl.BlockSpec(memory_space=pl.ANY),) * 2
        + (pl.BlockSpec(memory_space=pltpu.VMEM),) * 2,
        scratch_shapes=[
            pltpu.VMEM((2, XS, OWN, BLOCK), jnp.int32),
            pltpu.VMEM((LIST, BLOCK), jnp.int32),
            pltpu.VMEM((LIST, BLOCK), jnp.float32),
            pltpu.SMEM((LIST, BLOCK), jnp.int32),
            pltpu.SMEM((LIST, BLOCK), jnp.float32),
            pltpu.VMEM((2 * HALF, BLOCK), jnp.bfloat16),
            pltpu.VMEM((SHARD, WIDTH), jnp.bfloat16),
            pltpu.VMEM((SHARD, OWN_WIDTH), jnp.bfloat16),
            pltpu.VMEM((BANDS, OWN, BLOCK, BLOCK), jnp.float32),
            pltpu.VMEM((2 * CHIPS * BANDS, BLOCK), jnp.float32),
            pltpu.VMEM((WIDTH, OWN_WIDTH), jnp.bfloat16),
            pltpu.VMEM((WIDTH, OWN_WIDTH), jnp.bfloat16),
            pltpu.SemaphoreType.DMA((len(PLAN),)),
            pltpu.SemaphoreType.DMA,
            pltpu.SemaphoreType.DMA,
            pltpu.SemaphoreType.DMA,
            pltpu.SemaphoreType.DMA((ZS + YS,)),
            pltpu.SemaphoreType.DMA((ZS + YS,)),
            pltpu.SemaphoreType.DMA((2,)),
            pltpu.SemaphoreType.DMA((2,)),
        ],
        compiler_params=pltpu.CompilerParams(
            collective_id=0, has_side_effects=True, vmem_limit_bytes=60 * 2**20
        ),
    )(expression, jnp.transpose(nbr_owner, (0, 2, 1)), jnp.transpose(nbr_slot, (0, 2, 1)))

    steps = 2
    half = BANDS // steps
    tiles = pl.BlockSpec((half, OWN, BLOCK, BLOCK), lambda i: (i, 0, 0, 0))
    return pl.pallas_call(
        divide,
        out_shape=jax.ShapeDtypeStruct((BANDS, OWN, BLOCK, BLOCK), jnp.float32),
        grid=(steps,),
        in_specs=[
            tiles,
            pl.BlockSpec((half * BLOCK, OWN_WIDTH), lambda i: (i, 0)),
            pl.BlockSpec((half, BLOCK), lambda i: (i, 0)),
            pl.BlockSpec((half, OWN, BLOCK), lambda i: (i, 0, 0)),
        ],
        out_specs=tiles,
    )(sums, links, own, near)


def solution(mesh):
    return jax.shard_map(
        per_device,
        mesh=mesh,
        in_specs=(P("rows", None, None), P(), P()),
        out_specs=P("rows", "nbr", None, None),
        check_vma=False,
    )
```

```python
import heapq

import jax
import jax.numpy as jnp
from jax import lax
from jax.experimental import pallas as pl
from jax.experimental.pallas import tpu as pltpu
from jax.sharding import PartitionSpec as P

MESH = pl.DeviceIdType.MESH
BLOCK = 128
BANDS = 16
LIST = 16
OWN = 4
ZS, YS, XS = 8, 4, 4
CHIPS = ZS * YS
SHARD = BANDS * BLOCK
HALF = CHIPS * SHARD
ROWS = {("A", "a"): 304, ("A", "b"): 304, ("B", "a"): 384, ("B", "b"): 384, ("C", "a"): 384, ("C", "b"): 288}
EVEN = {("A", "a"): 0, ("A", "b"): 304, ("B", "a"): 608, ("B", "b"): 992, ("C", "a"): 608, ("C", "b"): 992}
ODD = {("A", "a"): 0, ("A", "b"): 304, ("B", "a"): 1664, ("B", "b"): 1280, ("C", "a"): 1664, ("C", "b"): 1376}
WIDTH = LIST * BLOCK + BLOCK
OWN_WIDTH = OWN * BLOCK
NT = (((1,), (1,)), ((), ()))


def next_sends(kind, part, dy, dz):
    sends = []
    if kind == "C":
        return sends
    along_z, along_y = [], []
    if 0 <= dz < 3:
        along_z.append(("z+", kind, part, dy, dz + 1))
    if dz == 3 and part == "a":
        along_z.append(("z+", kind, part, dy, 4))
    if -3 < dz <= 0:
        along_z.append(("z-", kind, part, dy, dz - 1))
    if dz == -3 and part == "b":
        along_z.append(("z-", kind, part, dy, -4))
    if dy == 0:
        along_y += [("y+", kind, part, 1, dz), ("y-", kind, part, -1, dz)]
    if dy == 1 and part == "a":
        along_y.append(("y+", kind, part, 2, dz))
    if dy == -1 and part == "b":
        along_y.append(("y-", kind, part, -2, dz))
    if kind == "A":
        sends += along_y if dz == 0 else []
        sends += along_z
    else:
        sends += along_z if dy == 0 else []
        sends += along_y
        if dy or dz:
            sends.append(("x+" if dz % 2 == 0 else "x-", "C", part, dy, dz))
    return sends


def gather_plan():
    free, heap, order, count, clock = {}, [], [], 0, 0.0
    for kind, part in (("B", "a"), ("B", "b"), ("A", "a"), ("A", "b")):
        heapq.heappush(heap, (0.0, count, (None, kind, part, 0, 0)))
        count += 1
    while heap:
        time, _, event = heapq.heappop(heap)
        order.append(event)
        clock = max(clock, time) + 0.1
        for send in next_sends(*event[1:]):
            began = max(free.get(send[0], 0.0), clock)
            free[send[0]] = began + 2 * ROWS[send[1:3]] * 256 / 95e3
            heapq.heappush(heap, (free[send[0]] + 3.2, count, send))
            count += 1
    return order


PLAN = gather_plan()
ARRIVALS = {event: number for number, event in enumerate(PLAN)}


def standardize_into(x_ref, z_all, mine):
    def four(step, carry):
        for i in range(4):
            block = 4 * step + i
            values = x_ref[block].astype(jnp.float32)
            centred = values - jnp.mean(values, axis=-1, keepdims=True)
            inverse = lax.rsqrt(jnp.sum(centred * centred, axis=-1, keepdims=True) + 1e-06)
            rows = pl.ds(pl.multiple_of(mine + block * BLOCK, BLOCK), BLOCK)
            z_all[rows, :] = (centred * inverse).astype(jnp.bfloat16)
        return carry

    lax.fori_loop(0, BANDS // 4, four, 0)


def list_blocks(row, plane, lists, blocks, weights):
    groups = [(plane + i) % XS for i in range(XS)]
    owner = jnp.concatenate([lists[0, group] for group in groups], axis=0)
    slot = jnp.concatenate([lists[1, group] for group in groups], axis=0)
    block = (owner & 1) * (CHIPS * BANDS) + (owner >> 1) * BANDS + slot
    lane = lax.broadcasted_iota(jnp.int32, (LIST, BLOCK), 1)
    place = lax.broadcasted_iota(jnp.int32, (LIST, BLOCK), 0)
    band_row = row // 8 * 8 + (lane >> 4)
    band = (band_row & 1) * (CHIPS * BANDS) + (band_row >> 1) * BANDS + (lane & 15)
    kept = jnp.where(block == band, 0.0, 1.0)
    for earlier in range(LIST - 1):
        repeats = (block == block[earlier : earlier + 1]) & (place > earlier)
        kept = jnp.where(repeats, 0.0, kept)
    blocks[...] = block
    weights[...] = kept


def off_diagonal(dtype):
    i = lax.broadcasted_iota(jnp.int32, (BLOCK, BLOCK), 0)
    j = lax.broadcasted_iota(jnp.int32, (BLOCK, BLOCK), 1)
    return jnp.where(i == j, 0.0, 1.0).astype(dtype)


def block_of(z_all, block):
    return z_all[pl.ds(block * BLOCK, BLOCK), :]


def lead_band(b, my_block, listed, weight, z_all, lead, own_tiles):
    band = block_of(z_all, my_block + b)
    left = band * jnp.bfloat16(0.5)
    at = pl.ds(pl.multiple_of(b * BLOCK, BLOCK), BLOCK)
    apart = off_diagonal(jnp.float32)
    total = jnp.zeros((BLOCK, BLOCK), jnp.float32)
    for begin, end in ((0, 5), (5, 9), (9, 13), (13, 17)):
        right = [
            band if u == 0 else block_of(z_all, listed(b, u - 1)) for u in range(begin, end)
        ]
        base = 0.5 + lax.dot_general(
            left, jnp.concatenate(right, axis=0), NT, preferred_element_type=jnp.float32
        )
        second = base * base
        fourth = second * second
        soft = fourth * fourth * fourth
        for u in range(begin, end):
            tile = soft[:, (u - begin) * BLOCK : (u - begin + 1) * BLOCK]
            if u == 0:
                tile = tile * apart
            else:
                if u <= OWN:
                    tile = tile * (1.0 - (1.0 - weight(b, u - 1)) * (1.0 - apart))
                    own_tiles[at, (u - 1) * BLOCK : u * BLOCK] = tile.astype(jnp.bfloat16)
                tile = tile * weight(b, u - 1)
            lead[at, u * BLOCK : (u + 1) * BLOCK] = tile.astype(jnp.bfloat16)
            total = total + tile
    return jnp.sum(jnp.transpose(total), axis=0, keepdims=True)


def fill_pair(b, listed, z_all, own_tiles, pair):
    at = pl.ds(pl.multiple_of(b * BLOCK, BLOCK), BLOCK)
    own = [block_of(z_all, listed(b, c)) for c in range(OWN)]
    right = jnp.concatenate(own, axis=0) * jnp.bfloat16(0.5)
    apart = off_diagonal(jnp.bfloat16)
    pair[0:BLOCK, :] = own_tiles[at, :]
    for u in range(0, LIST, OWN):
        left = jnp.concatenate([block_of(z_all, listed(b, u + i)) for i in range(OWN)], axis=0)
        base = 0.5 + lax.dot_general(left, right, NT, preferred_element_type=jnp.float32)
        second = base * base
        fourth = (second * second).astype(jnp.bfloat16)
        soft = fourth * fourth * fourth
        top = (u + 1) * BLOCK
        pair[top : top + OWN * BLOCK, :] = soft
        if u == 0:
            for c in range(OWN):
                tile = slice(c * BLOCK, (c + 1) * BLOCK)
                pair[top + c * BLOCK : top + (c + 1) * BLOCK, tile] = soft[tile, tile] * apart


def sum_band(b, lead, own_tiles, sums, pair):
    at = pl.ds(pl.multiple_of(b * BLOCK, BLOCK), BLOCK)
    shared = jnp.dot(lead[at, :], pair[...], preferred_element_type=jnp.float32)
    numerator = shared + own_tiles[at, :].astype(jnp.float32)
    for c in range(OWN):
        sums[b, c] = numerator[:, c * BLOCK : (c + 1) * BLOCK]


def divide(sum_ref, link_ref, own_ref, near_ref, out_ref):
    for b in range(sum_ref.shape[0]):
        own = jnp.transpose(jnp.broadcast_to(own_ref[b : b + 1, :], (BLOCK, BLOCK)))
        for c in range(OWN):
            tile = link_ref[b * BLOCK : (b + 1) * BLOCK, c * BLOCK : (c + 1) * BLOCK]
            link = tile.astype(jnp.float32)
            out_ref[b, c] = sum_ref[b, c] / (jnp.minimum(own, near_ref[b, c : c + 1, :]) + 1.0 - link)


def kernel(
    x_ref, owner_ref, slot_ref,
    sum_out, link_out, own_out, near_out,
    lists, blocks, weights, block_ref, weight_ref,
    z_all, lead, own_tiles, sums, degrees, pair, later_pair,
    piece_recv, piece_send, core_recv, core_send, degree_recv, degree_send, out_sem, list_sem,
):
    row = lax.axis_index("rows")
    plane = lax.axis_index("nbr")
    core, chip = row % 2, row // 2
    y, z = chip % YS, chip // YS
    odd = plane % 2

    def device(to_z, to_y):
        return (((to_z + ZS) % ZS * YS + (to_y + YS) % YS) * 2 + core, plane)

    links = {
        "z+": device(z + 1, y), "z-": device(z - 1, y),
        "y+": device(z, y + 1), "y-": device(z, y - 1),
        "x+": (row, (plane + 1) % XS), "x-": (row, (plane + XS - 1) % XS),
    }
    other = (chip * 2 + 1 - core, plane)
    along_z = {dz: device(z + dz, y) for dz in range(1, ZS)}
    along_y = {dy: device(z, y + dy) for dy in range(1, YS)}
    barrier = pltpu.get_barrier_semaphore()
    greeted = list(along_z.values()) + list(along_y.values()) + [links["x+"], links["x-"], other]
    for neighbour in greeted:
        pl.semaphore_signal(barrier, inc=1, device_id=neighbour, device_id_type=MESH)
    window = pl.ds(pl.multiple_of(row // 8 * BLOCK, BLOCK), BLOCK)
    list_copies = [
        pltpu.make_async_copy(ref.at[:, :, window], lists.at[i], list_sem.at[i])
        for i, ref in enumerate((owner_ref, slot_ref))
    ]
    for list_copy in list_copies:
        list_copy.start()
    mine = core * HALF + chip * SHARD
    standardize_into(x_ref, z_all, mine)
    pl.semaphore_wait(barrier, len(greeted))

    def rows_at(kind, part, dy, dz, parity):
        owner = (z - dz + ZS) % ZS * YS + (y - dy + YS) % YS
        first = core * HALF + owner * SHARD + EVEN[kind, part]
        apart = ODD[kind, part] - EVEN[kind, part]
        if apart:
            first = first + parity * apart
        return z_all.at[pl.ds(pl.multiple_of(first, 16), ROWS[kind, part])]

    def copy(ref, send, recv, to):
        return pltpu.make_async_remote_copy(
            src_ref=ref, dst_ref=ref, send_sem=send, recv_sem=recv, device_id=to, device_id_type=MESH
        )

    shard = z_all.at[pl.ds(pl.multiple_of(mine, SHARD), SHARD)]
    sent_rows = 0
    for number, event in enumerate(PLAN):
        link, kind, part, dy, dz = event
        ref = rows_at(kind, part, dy, dz, 1 - odd if kind == "C" else odd)
        if number == 4:
            for list_copy in list_copies:
                list_copy.wait()
            list_blocks(row, plane, lists, blocks, weights)
            number_copies = [
                pltpu.make_async_copy(blocks, block_ref, list_sem.at[0]),
                pltpu.make_async_copy(weights, weight_ref, list_sem.at[1]),
            ]
            for number_copy in number_copies:
                number_copy.start()
        if link is not None:
            copy(ref, piece_send, piece_recv.at[ARRIVALS[event]], links[link]).wait_recv()
        for send in next_sends(kind, part, dy, dz):
            sent_rows += ROWS[send[1:3]]
            sent = rows_at("C", part, dy, dz, odd) if send[1] == "C" else ref
            copy(sent, piece_send, piece_recv.at[ARRIVALS[send]], links[send[0]]).start()
        if link is not None:
            copy(ref, core_send, core_recv, other).start()
        elif kind == "A" and part == "b":
            copy(shard, core_send, core_recv, other).start()
    for number_copy in number_copies:
        number_copy.wait()
    first_lane = row % 8 * BANDS

    def listed(b, k):
        return block_ref[k, first_lane + b]

    def weight(b, k):
        return weight_ref[k, first_lane + b]

    def drain(sem, first, rows):
        ref = z_all.at[pl.ds(first, rows)]
        pltpu.make_async_copy(ref, ref, sem).wait()

    drain(core_recv, pl.multiple_of((1 - core) * HALF, HALF), HALF)

    my_degrees = mine // BLOCK

    def lead_step(step, carry):
        for i in range(4):
            b = 4 * step + i
            degrees[pl.ds(my_degrees + b, 1), :] = lead_band(
                b, mine // BLOCK, listed, weight, z_all, lead, own_tiles
            )
        return carry

    lax.fori_loop(0, BANDS // 4, lead_step, 0)
    link_copy = pltpu.make_async_copy(own_tiles, link_out, out_sem.at[1])
    link_copy.start()

    def emit(b):
        pltpu.make_async_copy(sums.at[b], sum_out.at[b], out_sem.at[0]).start()

    def of_device(dy):
        first = core * (CHIPS * BANDS) + (z * YS + (y - dy + YS) % YS) * BANDS
        return degrees.at[pl.ds(pl.multiple_of(first, BANDS), BANDS)]

    def of_line(dz):
        first = core * (CHIPS * BANDS) + (z - dz + ZS) % ZS * (YS * BANDS)
        return degrees.at[pl.ds(pl.multiple_of(first, YS * BANDS), YS * BANDS)]

    def of_core(which):
        return degrees.at[pl.ds(pl.multiple_of(which * (CHIPS * BANDS), CHIPS * BANDS), CHIPS * BANDS)]

    def passed(number, ref, to):
        return copy(ref, degree_send.at[number], degree_recv.at[number], to)

    def exchange(stage):
        if stage == 1:
            for dy in range(1, YS):
                passed(ZS + dy, of_device(dy), along_y[dy]).wait()
        if stage == 2:
            for dz in range(1, ZS):
                passed(dz, of_line(dz), along_z[dz]).wait()
        if stage == 3:
            passed(0, of_core(1 - core), other).wait()
        if stage == 0:
            for dy in range(1, YS):
                passed(ZS + dy, of_device(0), along_y[dy]).start()
        if stage == 1:
            for dz in range(1, ZS):
                passed(dz, of_line(0), along_z[dz]).start()
        if stage == 2:
            passed(0, of_core(core), other).start()

    fill_pair(0, listed, z_all, own_tiles, pair)

    def sum_step(step, carry):
        for stage in range(3):
            pl.when(step == 2 * stage)(lambda stage=stage: exchange(stage))
        b = 2 * step
        fill_pair(b + 1, listed, z_all, own_tiles, later_pair)
        sum_band(b, lead, own_tiles, sums, pair)
        fill_pair(b + 2, listed, z_all, own_tiles, pair)
        sum_band(b + 1, lead, own_tiles, sums, later_pair)
        emit(b)
        emit(b + 1)
        return carry

    lax.fori_loop(0, BANDS // 2 - 1, sum_step, 0)
    fill_pair(BANDS - 1, listed, z_all, own_tiles, later_pair)
    sum_band(BANDS - 2, lead, own_tiles, sums, pair)
    sum_band(BANDS - 1, lead, own_tiles, sums, later_pair)
    emit(BANDS - 2)
    emit(BANDS - 1)
    exchange(3)
    own_out[...] = degrees[pl.ds(pl.multiple_of(my_degrees, BANDS), BANDS), :]

    def near_step(b, carry):
        for c in range(OWN):
            near_out[b, c : c + 1, :] = degrees[pl.ds(listed(b, c), 1), :]
        return carry

    lax.fori_loop(0, BANDS, near_step, 0)
    link_copy.wait()
    pltpu.make_async_copy(sums, sum_out, out_sem.at[0]).wait()
    drain(piece_send, 0, sent_rows)
    drain(core_send, 0, HALF)


def per_device(expression, nbr_owner, nbr_slot):
    sums, links, own, near = pl.pallas_call(
        kernel,
        out_shape=(
            jax.ShapeDtypeStruct((BANDS, OWN, BLOCK, BLOCK), jnp.float32),
            jax.ShapeDtypeStruct((SHARD, OWN_WIDTH), jnp.bfloat16),
            jax.ShapeDtypeStruct((BANDS, BLOCK), jnp.float32),
            jax.ShapeDtypeStruct((BANDS, OWN, BLOCK), jnp.float32),
        ),
        in_specs=[pl.BlockSpec(memory_space=pltpu.VMEM)]
        + [pl.BlockSpec(memory_space=pl.ANY)] * 2,
        out_specs=(pl.BlockSpec(memory_space=pl.ANY),) * 2
        + (pl.BlockSpec(memory_space=pltpu.VMEM),) * 2,
        scratch_shapes=[
            pltpu.VMEM((2, XS, OWN, BLOCK), jnp.int32),
            pltpu.VMEM((LIST, BLOCK), jnp.int32),
            pltpu.VMEM((LIST, BLOCK), jnp.float32),
            pltpu.SMEM((LIST, BLOCK), jnp.int32),
            pltpu.SMEM((LIST, BLOCK), jnp.float32),
            pltpu.VMEM((2 * HALF, BLOCK), jnp.bfloat16),
            pltpu.VMEM((SHARD, WIDTH), jnp.bfloat16),
            pltpu.VMEM((SHARD, OWN_WIDTH), jnp.bfloat16),
            pltpu.VMEM((BANDS, OWN, BLOCK, BLOCK), jnp.float32),
            pltpu.VMEM((2 * CHIPS * BANDS, BLOCK), jnp.float32),
            pltpu.VMEM((WIDTH, OWN_WIDTH), jnp.bfloat16),
            pltpu.VMEM((WIDTH, OWN_WIDTH), jnp.bfloat16),
            pltpu.SemaphoreType.DMA((len(PLAN),)),
            pltpu.SemaphoreType.DMA,
            pltpu.SemaphoreType.DMA,
            pltpu.SemaphoreType.DMA,
            pltpu.SemaphoreType.DMA((ZS + YS,)),
            pltpu.SemaphoreType.DMA((ZS + YS,)),
            pltpu.SemaphoreType.DMA((2,)),
            pltpu.SemaphoreType.DMA((2,)),
        ],
        compiler_params=pltpu.CompilerParams(
            collective_id=0, has_side_effects=True, vmem_limit_bytes=60 * 2**20
        ),
    )(expression, jnp.transpose(nbr_owner, (0, 2, 1)), jnp.transpose(nbr_slot, (0, 2, 1)))

    steps = 2
    half = BANDS // steps
    tiles = pl.BlockSpec((half, OWN, BLOCK, BLOCK), lambda i: (i, 0, 0, 0))
    return pl.pallas_call(
        divide,
        out_shape=jax.ShapeDtypeStruct((BANDS, OWN, BLOCK, BLOCK), jnp.float32),
        grid=(steps,),
        in_specs=[
            tiles,
            pl.BlockSpec((half * BLOCK, OWN_WIDTH), lambda i: (i, 0)),
            pl.BlockSpec((half, BLOCK), lambda i: (i, 0)),
            pl.BlockSpec((half, OWN, BLOCK), lambda i: (i, 0, 0)),
        ],
        out_specs=tiles,
    )(sums, links, own, near)


def solution(mesh):
    return jax.shard_map(
        per_device,
        mesh=mesh,
        in_specs=(P("rows", None, None), P(), P()),
        out_specs=P("rows", "nbr", None, None),
        check_vma=False,
    )
```
